32 devices in a mesh: dp: 2 (over y), expert: 16 (over z, x, core).
Axes of the slice: x: 2, y: 2, z: 4, core: 2. Of those that a mesh axis runs over, the one named last changes fastest.
Arguments:
- cell_rows: bfloat16 [2, 4096, 1024], P(None, ('dp', 'expert')), may hold values from -6 to 6
- cotangent: bfloat16 [2, 4096, 1024], P(None, ('dp', 'expert')), may hold values from -0.75 to 0.75
- cluster_ids: int32 [2, 4096, 1], P(None, ('dp', 'expert')), may hold values from 0 to 15; in each aligned block of 128 rows (0 to 127, 128 to 255, ..., all dimensions but the last counted through in order) at most 8 rows name the same one
- enc_weight: bfloat16 [1024, 1024], replicated, may hold values from -0.1875 to 0.1875
- up_weight: bfloat16 [16, 1024, 2048], P('expert'), may hold values from -0.1875 to 0.1875
- down_weight: bfloat16 [16, 1024, 2048], P('expert'), may hold values from -0.125 to 0.125
Outputs:
- enc_grad: float32 [1024, 1024], P(('dp', 'expert'))
- up_grad: bfloat16 [16, 1024, 2048], P('expert', 'dp')
- down_grad: bfloat16 [16, 1024, 2048], P('expert', 'dp')
The draws below stay inside these ranges and needn't reach their ends.
Inputs may be any that keep to these rules, and one draw needn't show every extreme that they name: `cluster_ids`: in each micro-batch the 128 rows of one device name one cluster at most 8 times, a bound that some block reaches.
All inputs are finite; a program needn't handle non-finite values.
Results may differ from the reference program's by a relative error of at most 0.014.
Values may be sent and summed in bfloat16 or wider, within the bound.
No kernel may reach another device: no remote copies, remote signals or barrier semaphores. Data moves between devices by JAX's collectives and lax.ppermute only.
A program may use at most 128 MiB of HBM per device.

```python
import math
import jax
import jax.numpy as jnp
import numpy as np
from jax import lax

D = 1024
H = 2048
MICRO = 2
MB_ROWS = 128
CLUSTERS = 16
CAP = 8
TOKENS_MB = 4096
N_DP = 2
N_EXPERT = 16


def with_spikes(values, own_key, source, target, blocks, factor):
    def block_of(position):
        return (jnp.arange(values.shape[position]) // (values.shape[position] // blocks)).reshape((-1,) + (1,) * (values.ndim - 1 - position))

    one_side = jax.random.permutation(own_key, blocks)[block_of(target)]
    other_side = (block_of(target) + blocks // 2) % blocks
    return jnp.where((block_of(source) == one_side) | (block_of(source) == other_side), factor * values, values)


def block_levels(key, shape, pieces, smallest, top_value):
    gain = 1.0
    for axis_at, parts in pieces:
        draws = jax.random.uniform(jax.random.fold_in(jax.random.fold_in(key, 6), axis_at), (parts,), jnp.float32, smallest / len(pieces), top_value / len(pieces))
        gain = gain * jnp.repeat(jnp.exp(draws), shape[axis_at] // parts).reshape((-1,) + (1,) * (len(shape) - 1 - axis_at))
    return gain


def deal_out(stream_key, own, number, rows, count, top, bound, lean):
    order = jax.random.permutation(stream_key, count)
    packed, ordinary = shares(count, rows * top, bound, lean, True), shares(count, rows * top, bound, lean, False)
    places = jnp.arange(count)

    def named(tallies, offset_by):
        used = int((tallies > 0).sum())
        fixed = max(1, used // 4)
        passed = fixed + (places - fixed + offset_by * (used - fixed)) % max(1, count - fixed)
        return jnp.zeros((count,), jnp.int32).at[order[jnp.where(places < fixed, places, passed)]].set(jnp.asarray(tallies, jnp.int32))

    tallies = jnp.where(number % 4 == 0, named(packed, number // 4), named(ordinary, number - number // 4 - 1))
    mixed = jax.random.permutation(jax.random.fold_in(own, 3), count)
    giver, sink = mixed[0:count // 2 * 2:2], mixed[1:count // 2 * 2:2]
    room = jnp.minimum(tallies[giver] - 1, bound - tallies[sink]) // 2
    room = jnp.where((giver == order[0]) | (sink == order[0]) | (tallies[sink] == 0), 0, jnp.maximum(room, 0))
    passed = jax.random.randint(jax.random.fold_in(own, 4), (count // 2,), 0, 1 << 20) % (room + 1)
    tallies = tallies.at[giver].add(-passed).at[sink].add(passed)
    members = jnp.searchsorted(jnp.cumsum(tallies), jnp.arange(rows * top), side="right").astype(jnp.int32)
    table = members.reshape(top, rows).T
    table = table[jax.random.permutation(jax.random.fold_in(own, 1), rows)]
    offset_by = jax.random.randint(jax.random.fold_in(own, 2), (rows, 1), 0, top)
    return jnp.take_along_axis(table, (jnp.arange(top)[None, :] + offset_by) % top, axis=1)


def shares(number_of, total, reach, slope, full):
    loads = [(1 << 20) // math.isqrt(standing ** slope) + 1 for standing in range(1, number_of + 1)]
    largest = reach if full else min(reach, max(-(-total // number_of), total * loads[0] // sum(loads)))
    least = 1 if total - largest >= number_of - 1 else 0
    given, spare = [largest] + [least] * (number_of - 1), total - largest - least * (number_of - 1)
    while spare > 0:
        movable = [i for i in range(1, number_of) if given[i] < largest] or [i for i in range(1, number_of) if given[i] < reach]
        pool, left = sum([loads[i] for i in movable]), spare
        for i in movable:
            addition = min(reach - given[i], max(1, left * loads[i] // pool), spare)
            given[i] = given[i] + addition
            spare = spare - addition
    return np.array(given)


def noise(own_key, extent, width, reach, pieces=(), kind=jnp.bfloat16):
    result = width * jax.random.normal(own_key, extent, jnp.float32)
    if pieces:
        result = result * block_levels(own_key, extent, pieces, -0.22, 0.18)
    return jnp.clip(result, -reach, reach).astype(kind)


def heavy_noise(own_key, shape, deviation, most, pieces, heavy, held_as=jnp.bfloat16):
    values = deviation * jax.random.normal(own_key, shape, jnp.float32)
    if pieces:
        values = values * block_levels(own_key, shape, pieces, -0.22, 0.18)
    return jnp.clip(with_spikes(values, jax.random.fold_in(own_key, 3), *heavy), -most, most).astype(held_as)


def setup_inputs(seed: int = 0) -> dict:
    splits = jax.random.split(jax.random.key(seed), 7)
    cell_rows = heavy_noise(splits[0], (MICRO, TOKENS_MB, D), 1.0, 6.0, ((1, 32),), (1, 2, 32, 2.75))
    cotangent = noise(splits[1], (MICRO, TOKENS_MB, D), 0.05, 0.75, ((1, 32),))
    cluster_ids_keys = jax.random.split(jax.random.fold_in(splits[2], 1), MICRO * TOKENS_MB // MB_ROWS)
    cluster_ids_turns = jax.random.permutation(jax.random.fold_in(splits[2], 3), MICRO * TOKENS_MB // MB_ROWS)
    cluster_ids = jax.vmap(lambda own, number: deal_out(jax.random.fold_in(splits[2], 2), own, number, MB_ROWS, CLUSTERS, 1, CAP, 2))(cluster_ids_keys, cluster_ids_turns).reshape((MICRO, TOKENS_MB, 1))
    enc_weight = noise(splits[3], (D, D), D ** -0.5, 0.1875)
    up_weight = noise(splits[4], (CLUSTERS, D, H), D ** -0.5, 0.1875, ((0, 16),))
    down_weight = noise(splits[5], (CLUSTERS, D, H), H ** -0.5, 0.125, ((0, 16),))
    return {"cell_rows": cell_rows, "cotangent": cotangent, "cluster_ids": cluster_ids, "enc_weight": enc_weight, "up_weight": up_weight, "down_weight": down_weight}


epsilon = 1e-06

def silu_pair(pre_value):
    gate_value = jax.nn.sigmoid(pre_value)
    return (pre_value * gate_value, gate_value * (1.0 + pre_value * (1.0 - gate_value)))

def encode(features, enc_weight):
    pre_enc = jnp.dot(features, enc_weight, preferred_element_type=jnp.float32)
    silu_enc, slope_enc = silu_pair(pre_enc)
    encoded = features.astype(jnp.float32) + silu_enc
    inverse = lax.rsqrt(lax.optimization_barrier(jnp.mean(encoded * encoded, axis=-1, keepdims=True)) + epsilon)
    return (encoded, inverse, slope_enc)

def expert_pass(operands):
    norm_rows, grad_rows, w_up, w_down = operands
    norm_f32 = norm_rows.astype(jnp.float32)
    grad_f32 = grad_rows.astype(jnp.float32)
    up_f32 = w_up.astype(jnp.float32)
    pre_exp = jnp.einsum('drk,kh->drh', norm_f32, up_f32)
    silu_exp, slope_exp = silu_pair(pre_exp)
    active = silu_exp.astype(jnp.bfloat16)
    down_part = jnp.einsum('drk,drh->dkh', grad_f32, active.astype(jnp.float32)).astype(jnp.bfloat16)
    act_grad = jnp.einsum('drk,kh->drh', grad_f32, w_down.astype(jnp.float32))
    pre_grad = (act_grad * slope_exp).astype(jnp.bfloat16)
    up_part = jnp.einsum('drk,drh->dkh', norm_f32, pre_grad.astype(jnp.float32)).astype(jnp.bfloat16)
    back_rows = jnp.einsum('drh,kh->drk', pre_grad.astype(jnp.float32), up_f32).astype(jnp.bfloat16)
    up_sum = lax.optimization_barrier(jnp.sum(up_part.astype(jnp.float32), axis=0)).astype(jnp.bfloat16)
    down_sum = lax.optimization_barrier(jnp.sum(down_part.astype(jnp.float32), axis=0)).astype(jnp.bfloat16)
    return (up_sum, down_sum, back_rows)

def reference(cell_rows, cotangent, cluster_ids, enc_weight, up_weight, down_weight):
    devices_all = N_DP * N_EXPERT
    labels = cluster_ids[..., 0].astype(jnp.int32)
    blocks = labels.reshape(MICRO, devices_all, MB_ROWS)
    onehot = (blocks[..., None] == jnp.arange(CLUSTERS, dtype=jnp.int32)).astype(jnp.int32)
    before = (jnp.cumsum(onehot, axis=2) - onehot).astype(jnp.int32)
    slot_rank = lax.optimization_barrier(jnp.sum(before * onehot, axis=-1)).astype(jnp.int32)
    source = jnp.arange(devices_all, dtype=jnp.int32)
    dp_of = source // N_EXPERT
    ex_of = source % N_EXPERT
    per_batch = N_EXPERT * CAP
    bucket_rows = MICRO * per_batch
    batch_of = jnp.arange(MICRO, dtype=jnp.int32)
    target = ((blocks * N_DP + dp_of[None, :, None]) * bucket_rows + batch_of[:, None, None] * per_batch + ex_of[None, :, None] * CAP + slot_rank).reshape(-1).astype(jnp.int32)
    normed_list = []
    for batch_index in range(MICRO):
        encoded, inverse, slope_enc = encode(cell_rows[batch_index], enc_weight)
        normed_list.append((encoded * inverse).astype(jnp.bfloat16))
    normed_all = jnp.stack(normed_list).reshape(-1, D)
    slot_total = CLUSTERS * N_DP * bucket_rows
    sent_norm = jnp.zeros((slot_total, D), jnp.bfloat16).at[target].set(normed_all)
    sent_grad = jnp.zeros((slot_total, D), jnp.bfloat16).at[target].set(cotangent.reshape(-1, D))
    sent_norm = sent_norm.reshape(CLUSTERS, N_DP, bucket_rows, D)
    sent_grad = sent_grad.reshape(CLUSTERS, N_DP, bucket_rows, D)
    up_grad, down_grad, returned = lax.map(expert_pass, (sent_norm, sent_grad, up_weight, down_weight))
    norm_back = returned.reshape(slot_total, D)[target].reshape(MICRO, TOKENS_MB, D)
    enc_grad = jnp.zeros((D, D), jnp.float32)
    for batch_index in range(MICRO):
        encoded, inverse, slope_enc = encode(cell_rows[batch_index], enc_weight)
        norm_grad = norm_back[batch_index].astype(jnp.float32)
        enc_rows_grad = inverse * norm_grad - inverse * inverse * inverse * encoded * lax.optimization_barrier(jnp.mean(norm_grad * encoded, axis=-1, keepdims=True))
        enc_pre_grad = (enc_rows_grad * slope_enc).astype(jnp.bfloat16)
        enc_grad = enc_grad + jnp.dot(cell_rows[batch_index].T, enc_pre_grad, preferred_element_type=jnp.float32)
    return (enc_grad, up_grad, down_grad)
```

```python
import jax
import jax.numpy as jnp
from jax import lax
from jax.sharding import PartitionSpec as P

epsilon = 1e-06
contract_rows = (((0,), (0,)), ((), ()))
contract_last = (((1,), (1,)), ((), ()))


def silu_pair(pre_value):
    gate_value = jax.nn.sigmoid(pre_value)
    return (pre_value * gate_value, gate_value * (1.0 + pre_value * (1.0 - gate_value)))


def body(cell_rows, cotangent, cluster_ids, enc_weight, up_weight, down_weight):
    experts = lax.axis_size("expert")
    dp_count = lax.axis_size("dp")
    batch_count, local_rows, model_width = cell_rows.shape
    capacity = max(2, local_rows // 16)
    bucket = batch_count * capacity
    slot_count = experts * bucket
    w_up = up_weight[0]
    w_down = down_weight[0]

    labels = cluster_ids[:, :, 0]
    onehot = (labels[:, :, None] == jnp.arange(experts, dtype=jnp.int32)).astype(jnp.int32)
    slot_rank = jnp.sum((jnp.cumsum(onehot, axis=1) - onehot) * onehot, axis=2)
    batch_of = jnp.arange(batch_count, dtype=jnp.int32)[:, None]
    target = (labels * bucket + batch_of * capacity + slot_rank).reshape(-1)
    placer = (jnp.arange(slot_count, dtype=jnp.int32)[:, None] == target[None, :]).astype(
        jnp.bfloat16
    )

    def route(rows):
        placed = jnp.dot(
            placer, rows.reshape(-1, model_width), preferred_element_type=jnp.float32
        ).astype(jnp.bfloat16)
        return lax.all_to_all(
            placed.reshape(experts, bucket, model_width),
            "expert",
            split_axis=0,
            concat_axis=0,
            tiled=True,
        ).reshape(slot_count, model_width)

    def with_copies(rows):
        pieces = [rows]
        for shift in range(1, dp_count):
            ring = [(i, (i + shift) % dp_count) for i in range(dp_count)]
            pieces.append(lax.ppermute(rows, "dp", ring))
        return jnp.concatenate(pieces, axis=0)

    features = with_copies(route(cell_rows))
    grad_rows = with_copies(route(cotangent))

    pre_enc = jnp.dot(features, enc_weight, preferred_element_type=jnp.float32)
    silu_enc, slope_enc = silu_pair(pre_enc)
    encoded = features.astype(jnp.float32) + silu_enc
    inverse = lax.rsqrt(jnp.mean(encoded * encoded, axis=1, keepdims=True) + epsilon)
    norm_rows = (encoded * inverse).astype(jnp.bfloat16)

    pre_exp = jnp.dot(norm_rows, w_up, preferred_element_type=jnp.float32)
    silu_exp, slope_exp = silu_pair(pre_exp)
    active = silu_exp.astype(jnp.bfloat16)
    act_grad = jnp.dot(grad_rows, w_down, preferred_element_type=jnp.float32)
    pre_grad = (act_grad * slope_exp).astype(jnp.bfloat16)
    norm_grad = lax.dot_general(
        pre_grad, w_up, contract_last, preferred_element_type=jnp.float32
    )
    enc_rows_grad = inverse * norm_grad - inverse * inverse * inverse * encoded * jnp.mean(
        norm_grad * encoded, axis=1, keepdims=True
    )
    enc_pre_grad = (enc_rows_grad * slope_enc).astype(jnp.bfloat16)

    share = model_width // dp_count
    start = lax.axis_index("dp") * share

    def my_columns(rows):
        return lax.dynamic_slice_in_dim(rows, start, share, axis=1)

    enc_part = lax.dot_general(
        my_columns(features), enc_pre_grad, contract_rows, preferred_element_type=jnp.float32
    )
    enc_sum = lax.psum_scatter(
        enc_part.astype(jnp.bfloat16), "expert", scatter_dimension=0, tiled=True
    ).astype(jnp.float32)
    up_sum = lax.dot_general(
        my_columns(norm_rows), pre_grad, contract_rows, preferred_element_type=jnp.float32
    )
    down_sum = lax.dot_general(
        my_columns(grad_rows), active, contract_rows, preferred_element_type=jnp.float32
    )
    return (enc_sum, up_sum.astype(jnp.bfloat16)[None], down_sum.astype(jnp.bfloat16)[None])


def solution(mesh):
    in_specs = (
        P(None, ("dp", "expert"), None),
        P(None, ("dp", "expert"), None),
        P(None, ("dp", "expert"), None),
        P(),
        P("expert", None, None),
        P("expert", None, None),
    )
    out_specs = (P(("dp", "expert"), None), P("expert", "dp", None), P("expert", "dp", None))
    return jax.shard_map(body, mesh=mesh, in_specs=in_specs, out_specs=out_specs, check_vma=False)
```

```python
import jax
import jax.numpy as jnp
from jax import lax
from jax.sharding import PartitionSpec as P

epsilon = 1e-06
contract_rows = (((0,), (0,)), ((), ()))
contract_last = (((1,), (1,)), ((), ()))


def silu_pair(pre_value):
    gate_value = jax.nn.sigmoid(pre_value)
    return (pre_value * gate_value, gate_value * (1.0 + pre_value * (1.0 - gate_value)))


def body(cell_rows, cotangent, cluster_ids, enc_weight, up_weight, down_weight):
    experts = lax.axis_size("expert")
    dp_count = lax.axis_size("dp")
    batch_count, local_rows, model_width = cell_rows.shape
    capacity = max(2, local_rows // 16)
    bucket = batch_count * capacity
    slot_count = experts * bucket
    w_up = up_weight[0]
    w_down = down_weight[0]

    labels = cluster_ids[:, :, 0]
    onehot = (labels[:, :, None] == jnp.arange(experts, dtype=jnp.int32)).astype(jnp.int32)
    slot_rank = jnp.sum((jnp.cumsum(onehot, axis=1) - onehot) * onehot, axis=2)
    batch_of = jnp.arange(batch_count, dtype=jnp.int32)[:, None]
    target = (labels * bucket + batch_of * capacity + slot_rank).reshape(-1)
    placer = (jnp.arange(slot_count, dtype=jnp.int32)[:, None] == target[None, :]).astype(
        jnp.bfloat16
    )

    def route(rows):
        placed = jnp.dot(
            placer, rows.reshape(-1, model_width), preferred_element_type=jnp.float32
        ).astype(jnp.bfloat16)
        return lax.all_to_all(
            placed.reshape(experts, bucket, model_width),
            "expert",
            split_axis=0,
            concat_axis=0,
            tiled=True,
        ).reshape(slot_count, model_width)

    def copies(rows):
        pieces = [rows]
        for shift in range(1, dp_count):
            ring = [(i, (i + shift) % dp_count) for i in range(dp_count)]
            pieces.append(lax.ppermute(rows, "dp", ring))
        return pieces

    feature_parts = copies(route(cell_rows))
    grad_parts = copies(route(cotangent))

    share = model_width // dp_count
    start = lax.axis_index("dp") * share

    def my_columns(rows):
        return lax.dynamic_slice_in_dim(rows, start, share, axis=1)

    norm_parts, pre_grad_parts, active_parts = [], [], []
    enc_part = None
    for features, grad_rows in zip(feature_parts, grad_parts):
        pre_enc = jnp.dot(features, enc_weight, preferred_element_type=jnp.float32)
        silu_enc, slope_enc = silu_pair(pre_enc)
        encoded = features.astype(jnp.float32) + silu_enc
        inverse = lax.rsqrt(jnp.mean(encoded * encoded, axis=1, keepdims=True) + epsilon)
        norm_rows = (encoded * inverse).astype(jnp.bfloat16)
        pre_exp = jnp.dot(norm_rows, w_up, preferred_element_type=jnp.float32)
        silu_exp, slope_exp = silu_pair(pre_exp)
        active = silu_exp.astype(jnp.bfloat16)
        act_grad = jnp.dot(grad_rows, w_down, preferred_element_type=jnp.float32)
        pre_grad = (act_grad * slope_exp).astype(jnp.bfloat16)
        norm_grad = lax.dot_general(
            pre_grad, w_up, contract_last, preferred_element_type=jnp.float32
        )
        enc_rows_grad = inverse * norm_grad - inverse * inverse * inverse * encoded * jnp.mean(
            norm_grad * encoded, axis=1, keepdims=True
        )
        enc_pre_grad = (enc_rows_grad * slope_enc).astype(jnp.bfloat16)
        term = lax.dot_general(
            my_columns(features), enc_pre_grad, contract_rows, preferred_element_type=jnp.float32
        )
        enc_part = term if enc_part is None else enc_part + term
        norm_parts.append(my_columns(norm_rows))
        pre_grad_parts.append(pre_grad)
        active_parts.append(active)

    enc_sum = scatter_sum(enc_part)

    def rows_product(left, right):
        return lax.dot_general(
            jnp.concatenate(left, axis=0),
            jnp.concatenate(right, axis=0),
            contract_rows,
            preferred_element_type=jnp.float32,
        ).astype(jnp.bfloat16)

    up_sum = rows_product(norm_parts, pre_grad_parts)
    down_sum = rows_product([my_columns(g) for g in grad_parts], active_parts)
    return (enc_sum, up_sum[None], down_sum[None])


def scatter_sum(part):
    experts = lax.axis_size("expert")
    if experts & (experts - 1):
        return lax.psum_scatter(
            part.astype(jnp.bfloat16), "expert", scatter_dimension=0, tiled=True
        ).astype(jnp.float32)
    me = lax.axis_index("expert")
    width = part.shape[1]
    group, low = experts, 0
    part = part.reshape(experts, -1, width)
    while group > 4:
        bit = (me >> low) & 1
        pairs = part.reshape(group // 2, 2, -1, width)
        mine = lax.dynamic_slice_in_dim(pairs, bit, 1, axis=1)[:, 0]
        other = lax.dynamic_slice_in_dim(pairs, 1 - bit, 1, axis=1)[:, 0]
        swap = [(i, i ^ (1 << low)) for i in range(experts)]
        got = lax.ppermute(other.astype(jnp.bfloat16), "expert", swap)
        part = mine + got.astype(jnp.float32)
        group, low = group // 2, low + 1
    high = me >> low
    total = lax.dynamic_slice_in_dim(part, high, 1, axis=0)[0]
    sent = part.astype(jnp.bfloat16)
    for step in range(1, group):
        swap = [(i, i ^ (step << low)) for i in range(experts)]
        piece = lax.dynamic_slice_in_dim(sent, high ^ step, 1, axis=0)[0]
        total = total + lax.ppermute(piece, "expert", swap).astype(jnp.float32)
    return total


def solution(mesh):
    in_specs = (
        P(None, ("dp", "expert"), None),
        P(None, ("dp", "expert"), None),
        P(None, ("dp", "expert"), None),
        P(),
        P("expert", None, None),
        P("expert", None, None),
    )
    out_specs = (P(("dp", "expert"), None), P("expert", "dp", None), P("expert", "dp", None))
    return jax.shard_map(body, mesh=mesh, in_specs=in_specs, out_specs=out_specs, check_vma=False)
```

```python
import jax
import jax.numpy as jnp
from jax import lax
from jax.sharding import PartitionSpec as P

epsilon = 1e-06
contract_rows = (((0,), (0,)), ((), ()))
contract_last = (((1,), (1,)), ((), ()))


def silu_pair(pre_value):
    gate_value = jax.nn.sigmoid(pre_value)
    return (pre_value * gate_value, gate_value * (1.0 + pre_value * (1.0 - gate_value)))


def body(cell_rows, cotangent, cluster_ids, enc_weight, up_weight, down_weight):
    experts = lax.axis_size("expert")
    dp_count = lax.axis_size("dp")
    batch_count, local_rows, model_width = cell_rows.shape
    capacity = max(2, local_rows // 16)
    bucket = batch_count * capacity
    slot_count = experts * bucket
    w_up = up_weight[0]
    w_down = down_weight[0]

    high = min(4, experts)
    low = experts // high
    me = lax.axis_index("expert")
    labels = cluster_ids[:, :, 0]
    onehot = (labels[:, :, None] == jnp.arange(experts, dtype=jnp.int32)).astype(jnp.int32)
    slot_rank = jnp.sum((jnp.cumsum(onehot, axis=1) - onehot) * onehot, axis=2)
    batch_of = jnp.arange(batch_count, dtype=jnp.int32)[:, None]
    away = labels ^ me
    place = (away % low) * high + away // low
    target = (place * bucket + batch_of * capacity + slot_rank).reshape(-1)
    placer = (jnp.arange(slot_count, dtype=jnp.int32)[:, None] == target[None, :]).astype(
        jnp.bfloat16
    )

    def swap(piece, distance):
        pairs = [(i, i ^ distance) for i in range(experts)]
        return lax.ppermute(piece, "expert", pairs)

    def route(rows):
        placed = jnp.dot(
            placer, rows.reshape(-1, model_width), preferred_element_type=jnp.float32
        ).astype(jnp.bfloat16)
        placed = placed.reshape(low, high, bucket, model_width)
        near = jnp.stack(
            [placed[0]] + [swap(placed[step], step) for step in range(1, low)], axis=1
        )
        far = [near[0]] + [swap(near[step], step * low) for step in range(1, high)]
        return jnp.concatenate(far, axis=0).reshape(slot_count, model_width)

    def copies(rows):
        pieces = [rows]
        for shift in range(1, dp_count):
            ring = [(i, (i + shift) % dp_count) for i in range(dp_count)]
            pieces.append(lax.ppermute(rows, "dp", ring))
        return pieces

    feature_parts = copies(route(cell_rows))
    grad_parts = copies(route(cotangent))

    share = model_width // dp_count
    start = lax.axis_index("dp") * share

    def my_columns(rows):
        return lax.dynamic_slice_in_dim(rows, start, share, axis=1)

    norm_parts, pre_grad_parts, active_parts = [], [], []
    enc_part = None
    for features, grad_rows in zip(feature_parts, grad_parts):
        pre_enc = jnp.dot(features, enc_weight, preferred_element_type=jnp.float32)
        silu_enc, slope_enc = silu_pair(pre_enc)
        encoded = features.astype(jnp.float32) + silu_enc
        inverse = lax.rsqrt(jnp.mean(encoded * encoded, axis=1, keepdims=True) + epsilon)
        norm_rows = (encoded * inverse).astype(jnp.bfloat16)
        pre_exp = jnp.dot(norm_rows, w_up, preferred_element_type=jnp.float32)
        silu_exp, slope_exp = silu_pair(pre_exp)
        active = silu_exp.astype(jnp.bfloat16)
        act_grad = jnp.dot(grad_rows, w_down, preferred_element_type=jnp.float32)
        pre_grad = (act_grad * slope_exp).astype(jnp.bfloat16)
        norm_grad = lax.dot_general(
            pre_grad, w_up, contract_last, preferred_element_type=jnp.float32
        )
        enc_rows_grad = inverse * norm_grad - inverse * inverse * inverse * encoded * jnp.mean(
            norm_grad * encoded, axis=1, keepdims=True
        )
        enc_pre_grad = (enc_rows_grad * slope_enc).astype(jnp.bfloat16)
        term = lax.dot_general(
            my_columns(features), enc_pre_grad, contract_rows, preferred_element_type=jnp.float32
        )
        enc_part = term if enc_part is None else enc_part + term
        norm_parts.append(my_columns(norm_rows))
        pre_grad_parts.append(pre_grad)
        active_parts.append(active)

    enc_sum = scatter_sum(enc_part)

    def rows_product(left, right):
        return lax.dot_general(
            jnp.concatenate(left, axis=0),
            jnp.concatenate(right, axis=0),
            contract_rows,
            preferred_element_type=jnp.float32,
        ).astype(jnp.bfloat16)

    up_sum = rows_product(norm_parts, pre_grad_parts)
    down_sum = rows_product([my_columns(g) for g in grad_parts], active_parts)
    return (enc_sum, up_sum[None], down_sum[None])


def scatter_sum(part):
    experts = lax.axis_size("expert")
    if experts & (experts - 1):
        return lax.psum_scatter(
            part.astype(jnp.bfloat16), "expert", scatter_dimension=0, tiled=True
        ).astype(jnp.float32)
    me = lax.axis_index("expert")
    width = part.shape[1]
    group, low = experts, 0
    part = part.reshape(experts, -1, width)
    while group > 4:
        bit = (me >> low) & 1
        pairs = part.reshape(group // 2, 2, -1, width)
        mine = lax.dynamic_slice_in_dim(pairs, bit, 1, axis=1)[:, 0]
        other = lax.dynamic_slice_in_dim(pairs, 1 - bit, 1, axis=1)[:, 0]
        swap = [(i, i ^ (1 << low)) for i in range(experts)]
        got = lax.ppermute(other.astype(jnp.bfloat16), "expert", swap)
        part = mine + got.astype(jnp.float32)
        group, low = group // 2, low + 1
    high = me >> low
    total = lax.dynamic_slice_in_dim(part, high, 1, axis=0)[0]
    sent = part.astype(jnp.bfloat16)
    for step in range(1, group):
        swap = [(i, i ^ (step << low)) for i in range(experts)]
        piece = lax.dynamic_slice_in_dim(sent, high ^ step, 1, axis=0)[0]
        total = total + lax.ppermute(piece, "expert", swap).astype(jnp.float32)
    return total


def solution(mesh):
    in_specs = (
        P(None, ("dp", "expert"), None),
        P(None, ("dp", "expert"), None),
        P(None, ("dp", "expert"), None),
        P(),
        P("expert", None, None),
        P("expert", None, None),
    )
    out_specs = (P(("dp", "expert"), None), P("expert", "dp", None), P("expert", "dp", None))
    return jax.shard_map(body, mesh=mesh, in_specs=in_specs, out_specs=out_specs, check_vma=False)
```

```python
import jax
import jax.numpy as jnp
from jax import lax
from jax.sharding import PartitionSpec as P

epsilon = 1e-06
contract_rows = (((0,), (0,)), ((), ()))
contract_last = (((1,), (1,)), ((), ()))


def silu_pair(pre_value):
    gate_value = jax.nn.sigmoid(pre_value)
    return (pre_value * gate_value, gate_value * (1.0 + pre_value * (1.0 - gate_value)))


def body(cell_rows, cotangent, cluster_ids, enc_weight, up_weight, down_weight):
    experts = lax.axis_size("expert")
    dp_count = lax.axis_size("dp")
    batch_count, local_rows, model_width = cell_rows.shape
    capacity = max(2, local_rows // 16)
    bucket = batch_count * capacity
    slot_count = experts * bucket
    w_up = up_weight[0]
    w_down = down_weight[0]

    high = min(4, experts)
    low = experts // high
    me = lax.axis_index("expert")
    labels = cluster_ids[:, :, 0]
    onehot = (labels[:, :, None] == jnp.arange(experts, dtype=jnp.int32)).astype(jnp.int32)
    slot_rank = jnp.sum((jnp.cumsum(onehot, axis=1) - onehot) * onehot, axis=2)
    batch_of = jnp.arange(batch_count, dtype=jnp.int32)[:, None]
    away = labels ^ me
    place = (away % low) * high + away // low
    target = (place * bucket + batch_of * capacity + slot_rank).reshape(-1)
    placer = (jnp.arange(slot_count, dtype=jnp.int32)[:, None] == target[None, :]).astype(
        jnp.bfloat16
    )

    def swap(piece, distance):
        pairs = [(i, i ^ distance) for i in range(experts)]
        return lax.ppermute(piece, "expert", pairs)

    def place_near(rows):
        placed = jnp.dot(
            placer, rows.reshape(-1, model_width), preferred_element_type=jnp.float32
        ).astype(jnp.bfloat16)
        placed = placed.reshape(low, high, bucket, model_width)
        return jnp.stack(
            [placed[0]] + [swap(placed[step], step) for step in range(1, low)], axis=1
        )

    def send_far(near):
        far = [near[0]] + [swap(near[step], step * low) for step in range(1, high)]
        rows = [piece.reshape(-1, model_width) for piece in far]
        half = (high + 1) // 2
        return jnp.concatenate(rows[:half], axis=0), jnp.concatenate(rows[half:], axis=0)

    def copies(rows):
        pieces = []
        for shift in range(1, dp_count):
            ring = [(i, (i + shift) % dp_count) for i in range(dp_count)]
            pieces.append(lax.ppermute(rows, "dp", ring))
        return pieces

    def with_copies(first, second):
        return [jnp.concatenate(pair, axis=0) for pair in
                [(first, second)] + list(zip(copies(first), copies(second)))]

    def silu_parts(features):
        pre_enc = jnp.dot(features, enc_weight, preferred_element_type=jnp.float32)
        silu_enc, slope_enc = silu_pair(pre_enc)
        encoded = features.astype(jnp.float32) + silu_enc
        inverse = lax.rsqrt(jnp.mean(encoded * encoded, axis=1, keepdims=True) + epsilon)
        norm_rows = (encoded * inverse).astype(jnp.bfloat16)
        pre_exp = jnp.dot(norm_rows, w_up, preferred_element_type=jnp.float32)
        silu_exp, slope_exp = silu_pair(pre_exp)
        return encoded, inverse, slope_enc, norm_rows, silu_exp.astype(jnp.bfloat16), slope_exp

    cells_near = place_near(cell_rows)
    grads_near = place_near(cotangent)
    cells_first, cells_second = send_far(cells_near)
    grads_near, cells_second = lax.optimization_barrier((grads_near, cells_second))
    grads_first, grads_second = send_far(grads_near)
    feature_parts = with_copies(cells_first, cells_second)
    forward_parts = [silu_parts(features) for features in feature_parts]
    if dp_count <= 2:
        grads_second, forward_parts = lax.optimization_barrier((grads_second, forward_parts))
    grad_parts = with_copies(grads_first, grads_second)

    share = model_width // dp_count
    start = lax.axis_index("dp") * share

    def my_columns(rows):
        return lax.dynamic_slice_in_dim(rows, start, share, axis=1)

    norm_parts, pre_grad_parts, active_parts = [], [], []
    enc_part = None
    for features, grad_rows, forward in zip(feature_parts, grad_parts, forward_parts):
        encoded, inverse, slope_enc, norm_rows, active, slope_exp = forward
        act_grad = jnp.dot(grad_rows, w_down, preferred_element_type=jnp.float32)
        pre_grad = (act_grad * slope_exp).astype(jnp.bfloat16)
        norm_grad = lax.dot_general(
            pre_grad, w_up, contract_last, preferred_element_type=jnp.float32
        )
        enc_rows_grad = inverse * norm_grad - inverse * inverse * inverse * encoded * jnp.mean(
            norm_grad * encoded, axis=1, keepdims=True
        )
        enc_pre_grad = (enc_rows_grad * slope_enc).astype(jnp.bfloat16)
        term = lax.dot_general(
            my_columns(features), enc_pre_grad, contract_rows, preferred_element_type=jnp.float32
        )
        enc_part = term if enc_part is None else enc_part + term
        norm_parts.append(my_columns(norm_rows))
        pre_grad_parts.append(pre_grad)
        active_parts.append(active)

    enc_sum = scatter_sum(enc_part)

    def rows_product(left, right):
        return lax.dot_general(
            jnp.concatenate(left, axis=0),
            jnp.concatenate(right, axis=0),
            contract_rows,
            preferred_element_type=jnp.float32,
        ).astype(jnp.bfloat16)

    up_sum = rows_product(norm_parts, pre_grad_parts)
    down_sum = rows_product([my_columns(g) for g in grad_parts], active_parts)
    return (enc_sum, up_sum[None], down_sum[None])


def scatter_sum(part):
    experts = lax.axis_size("expert")
    if experts & (experts - 1):
        return lax.psum_scatter(
            part.astype(jnp.bfloat16), "expert", scatter_dimension=0, tiled=True
        ).astype(jnp.float32)
    me = lax.axis_index("expert")
    width = part.shape[1]
    group, low = experts, 0
    part = part.reshape(experts, -1, width)
    while group > 4:
        bit = (me >> low) & 1
        pairs = part.reshape(group // 2, 2, -1, width)
        mine = lax.dynamic_slice_in_dim(pairs, bit, 1, axis=1)[:, 0]
        other = lax.dynamic_slice_in_dim(pairs, 1 - bit, 1, axis=1)[:, 0]
        swap = [(i, i ^ (1 << low)) for i in range(experts)]
        got = lax.ppermute(other.astype(jnp.bfloat16), "expert", swap)
        part = mine + got.astype(jnp.float32)
        group, low = group // 2, low + 1
    high = me >> low
    total = lax.dynamic_slice_in_dim(part, high, 1, axis=0)[0]
    sent = part.astype(jnp.bfloat16)
    for step in range(1, group):
        swap = [(i, i ^ (step << low)) for i in range(experts)]
        piece = lax.dynamic_slice_in_dim(sent, high ^ step, 1, axis=0)[0]
        total = total + lax.ppermute(piece, "expert", swap).astype(jnp.float32)
    return total


def solution(mesh):
    in_specs = (
        P(None, ("dp", "expert"), None),
        P(None, ("dp", "expert"), None),
        P(None, ("dp", "expert"), None),
        P(),
        P("expert", None, None),
        P("expert", None, None),
    )
    out_specs = (P(("dp", "expert"), None), P("expert", "dp", None), P("expert", "dp", None))
    return jax.shard_map(body, mesh=mesh, in_specs=in_specs, out_specs=out_specs, check_vma=False)
```

```python
import functools

import jax
import jax.numpy as jnp
from jax import lax
from jax.experimental import pallas as pl
from jax.experimental.pallas import tpu as pltpu
from jax.sharding import PartitionSpec as P

epsilon = 1e-06
contract_rows = (((0,), (0,)), ((), ()))
contract_last = (((1,), (1,)), ((), ()))


def silu_pair(pre_value):
    gate_value = jax.nn.sigmoid(pre_value)
    return (pre_value * gate_value, gate_value * (1.0 + pre_value * (1.0 - gate_value)))


def swap(piece, distance):
    pairs = [(i, i ^ distance) for i in range(lax.axis_size("expert"))]
    return lax.ppermute(piece, "expert", pairs)


def after(value, *others):
    return lax.optimization_barrier((value,) + others)[0]


def place_kernel(experts, low, high, capacity, me_ref, ids_ref, rows_ref, placer_ref, placed_ref):
    batches, rows = ids_ref.shape
    bucket = batches * capacity
    slots = experts * bucket
    earlier = (
        lax.broadcasted_iota(jnp.int32, (rows, rows), 0)
        < lax.broadcasted_iota(jnp.int32, (rows, rows), 1)
    )
    earlier = jnp.where(earlier, 1.0, 0.0).astype(jnp.bfloat16)
    for batch_index in range(batches):
        label = ids_ref[batch_index : batch_index + 1, :]
        named = lax.broadcasted_iota(jnp.int32, (experts, rows), 0) == label
        onehot = jnp.where(named, 1.0, 0.0)
        before = jnp.dot(onehot.astype(jnp.bfloat16), earlier, preferred_element_type=jnp.float32)
        rank = jnp.sum(before * onehot, axis=0, keepdims=True).astype(jnp.int32)
        away = label ^ me_ref[0]
        place = (away & (low - 1)) * high + (away >> (low.bit_length() - 1))
        slot = place * bucket + batch_index * capacity + rank
        hit = lax.broadcasted_iota(jnp.int32, (slots, rows), 0) == slot
        placer_ref[:, batch_index * rows : (batch_index + 1) * rows] = jnp.where(
            hit, 1.0, 0.0
        ).astype(jnp.bfloat16)
    placed_ref[...] = jnp.dot(
        placer_ref[...], rows_ref[...], preferred_element_type=jnp.float32
    ).astype(jnp.bfloat16)


def body(cell_rows, cotangent, cluster_ids, enc_weight, up_weight, down_weight):
    experts = lax.axis_size("expert")
    dp_count = lax.axis_size("dp")
    me = lax.axis_index("expert")
    batch_count, local_rows, model_width = cell_rows.shape
    capacity = max(2, local_rows // 16)
    bucket = batch_count * capacity
    slot_count = experts * bucket
    all_rows = batch_count * local_rows
    high = min(4, experts)
    low = experts // high
    w_up = up_weight[0]
    w_down = down_weight[0]

    vmem = pl.BlockSpec(memory_space=pltpu.VMEM)
    placer, placed_cells = pl.pallas_call(
        functools.partial(place_kernel, experts, low, high, capacity),
        out_shape=(
            jax.ShapeDtypeStruct((slot_count, all_rows), jnp.bfloat16),
            jax.ShapeDtypeStruct((slot_count, model_width), jnp.bfloat16),
        ),
        in_specs=[pl.BlockSpec(memory_space=pltpu.SMEM), vmem, vmem],
        out_specs=(vmem, vmem),
    )(me.astype(jnp.int32)[None], cluster_ids[:, :, 0], cell_rows.reshape(all_rows, model_width))
    placed_grads = jnp.dot(
        placer, cotangent.reshape(all_rows, model_width), preferred_element_type=jnp.float32
    ).astype(jnp.bfloat16)

    def send_near(placed):
        placed = placed.reshape(low, high, bucket, model_width)
        return jnp.stack(
            [placed[0]] + [swap(placed[step], step) for step in range(1, low)], axis=1
        )

    def send_far(near):
        far = [near[0]] + [swap(near[step], step * low) for step in range(1, high)]
        rows = [piece.reshape(-1, model_width) for piece in far]
        half = (high + 1) // 2
        return jnp.concatenate(rows[:half], axis=0), jnp.concatenate(rows[half:], axis=0)

    def copies(rows):
        pieces = []
        for shift in range(1, dp_count):
            ring = [(i, (i + shift) % dp_count) for i in range(dp_count)]
            pieces.append(lax.ppermute(rows, "dp", ring))
        return pieces

    def joined(first, second):
        return [jnp.concatenate(pair, axis=0) for pair in zip(first, second)]

    def forward(features):
        pre_enc = jnp.dot(features, enc_weight, preferred_element_type=jnp.float32)
        silu_enc, slope_enc = silu_pair(pre_enc)
        encoded = features.astype(jnp.float32) + silu_enc
        inverse = lax.rsqrt(jnp.mean(encoded * encoded, axis=1, keepdims=True) + epsilon)
        norm_rows = (encoded * inverse).astype(jnp.bfloat16)
        pre_exp = jnp.dot(norm_rows, w_up, preferred_element_type=jnp.float32)
        silu_exp, slope_exp = silu_pair(pre_exp)
        return encoded, inverse, slope_enc, norm_rows, silu_exp.astype(jnp.bfloat16), slope_exp

    cells_near = send_near(placed_cells)
    grads_near = send_near(after(placed_grads, cells_near))
    cells_first, cells_second = send_far(cells_near)
    grads_first, grads_second = send_far(grads_near)
    cells_first_copies = copies(cells_first)
    cells_second_copies = copies(after(cells_second, *cells_first_copies))
    features = joined([cells_first], [cells_second])[0]
    own_forward = forward(features)
    grads_first_copies = copies(grads_first)
    grads_second_copies = copies(after(grads_second, own_forward[4], *grads_first_copies))
    feature_parts = [features] + joined(cells_first_copies, cells_second_copies)
    forward_parts = [own_forward] + [forward(rows) for rows in feature_parts[1:]]
    grad_parts = joined([grads_first], [grads_second]) + joined(
        grads_first_copies, grads_second_copies
    )

    share = model_width // dp_count
    start = lax.axis_index("dp") * share
    block = share // experts

    def my_columns(rows):
        return lax.dynamic_slice_in_dim(rows, start, share, axis=1)

    stages = low.bit_length() - 1
    column = jnp.arange(share, dtype=jnp.int32)
    rank = column // block
    away = rank & (high - 1)
    away = away << stages
    for stage in range(stages):
        away = away | (((rank // high) >> (stages - 1 - stage)) & 1) << stage
    wanted = start + (away ^ me) * block + column % block
    picker = (jnp.arange(model_width, dtype=jnp.int32)[:, None] == wanted[None, :]).astype(
        jnp.bfloat16
    )

    norm_parts, pre_grad_parts, active_parts = [], [], []
    enc_parts = []
    for features, grad_rows, values in zip(feature_parts, grad_parts, forward_parts):
        encoded, inverse, slope_enc, norm_rows, active, slope_exp = values
        act_grad = jnp.dot(grad_rows, w_down, preferred_element_type=jnp.float32)
        pre_grad = (act_grad * slope_exp).astype(jnp.bfloat16)
        norm_grad = lax.dot_general(
            pre_grad, w_up, contract_last, preferred_element_type=jnp.float32
        )
        enc_rows_grad = inverse * norm_grad - inverse * inverse * inverse * encoded * jnp.mean(
            norm_grad * encoded, axis=1, keepdims=True
        )
        enc_pre_grad = (enc_rows_grad * slope_enc).astype(jnp.bfloat16)
        picked = jnp.dot(features, picker, preferred_element_type=jnp.float32).astype(jnp.bfloat16)
        enc_parts.append((picked, enc_pre_grad))
        norm_parts.append(my_columns(norm_rows))
        pre_grad_parts.append(pre_grad)
        active_parts.append(active)

    def enc_terms(first, last):
        total = None
        for picked, enc_pre_grad in enc_parts:
            term = lax.dot_general(
                picked[:, first:last],
                enc_pre_grad,
                contract_rows,
                preferred_element_type=jnp.float32,
            )
            total = term if total is None else total + term
        return total

    kept = share
    total = None
    for stage in range(stages):
        kept //= 2
        if total is None:
            sent, total = enc_terms(kept, 2 * kept), enc_terms(0, kept)
        else:
            sent, total = total[kept:], total[:kept]
        total = total + swap(sent.astype(jnp.bfloat16), 1 << stage).astype(jnp.float32)
    if total is None:
        total = enc_terms(0, share)
    sent = total.astype(jnp.bfloat16)
    total = total[:block]
    for step in range(1, high):
        piece = sent[step * block : (step + 1) * block]
        total = total + swap(piece, step * low).astype(jnp.float32)

    def rows_product(left, right):
        return lax.dot_general(
            jnp.concatenate(left, axis=0),
            jnp.concatenate(right, axis=0),
            contract_rows,
            preferred_element_type=jnp.float32,
        ).astype(jnp.bfloat16)

    up_sum = rows_product(norm_parts, pre_grad_parts)
    down_sum = rows_product([my_columns(g) for g in grad_parts], active_parts)
    return (total, up_sum[None], down_sum[None])


def solution(mesh):
    in_specs = (
        P(None, ("dp", "expert"), None),
        P(None, ("dp", "expert"), None),
        P(None, ("dp", "expert"), None),
        P(),
        P("expert", None, None),
        P("expert", None, None),
    )
    out_specs = (P(("dp", "expert"), None), P("expert", "dp", None), P("expert", "dp", None))
    return jax.shard_map(body, mesh=mesh, in_specs=in_specs, out_specs=out_specs, check_vma=False)
```

```python
import functools

import jax
import jax.numpy as jnp
from jax import lax
from jax.experimental import pallas as pl
from jax.experimental.pallas import tpu as pltpu
from jax.sharding import PartitionSpec as P

epsilon = 1e-06
contract_rows = (((0,), (0,)), ((), ()))
contract_last = (((1,), (1,)), ((), ()))


def silu_pair(pre_value):
    gate_value = jax.nn.sigmoid(pre_value)
    return (pre_value * gate_value, gate_value * (1.0 + pre_value * (1.0 - gate_value)))


def swap(piece, distance):
    pairs = [(i, i ^ distance) for i in range(lax.axis_size("expert"))]
    return lax.ppermute(piece, "expert", pairs)


def place_kernel(experts, low, high, capacity, me_ref, ids_ref, rows_ref, placer_ref, placed_ref):
    batches, rows = ids_ref.shape
    bucket = batches * capacity
    slots = experts * bucket
    earlier = (
        lax.broadcasted_iota(jnp.int32, (rows, rows), 0)
        < lax.broadcasted_iota(jnp.int32, (rows, rows), 1)
    )
    earlier = jnp.where(earlier, 1.0, 0.0).astype(jnp.bfloat16)
    for batch_index in range(batches):
        label = ids_ref[batch_index : batch_index + 1, :]
        named = lax.broadcasted_iota(jnp.int32, (experts, rows), 0) == label
        onehot = jnp.where(named, 1.0, 0.0)
        before = jnp.dot(onehot.astype(jnp.bfloat16), earlier, preferred_element_type=jnp.float32)
        rank = jnp.sum(before * onehot, axis=0, keepdims=True).astype(jnp.int32)
        away = label ^ me_ref[0]
        place = (away & (low - 1)) * high + (away >> (low.bit_length() - 1))
        slot = place * bucket + batch_index * capacity + rank
        hit = lax.broadcasted_iota(jnp.int32, (slots, rows), 0) == slot
        placer_ref[:, batch_index * rows : (batch_index + 1) * rows] = jnp.where(
            hit, 1.0, 0.0
        ).astype(jnp.bfloat16)
    placed_ref[...] = jnp.dot(
        placer_ref[...], rows_ref[...], preferred_element_type=jnp.float32
    ).astype(jnp.bfloat16)


def body(cell_rows, cotangent, cluster_ids, enc_weight, up_weight, down_weight):
    experts = lax.axis_size("expert")
    dp_count = lax.axis_size("dp")
    me = lax.axis_index("expert")
    batch_count, local_rows, model_width = cell_rows.shape
    capacity = max(2, local_rows // 16)
    bucket = batch_count * capacity
    slot_count = experts * bucket
    all_rows = batch_count * local_rows
    high = min(4, experts)
    low = experts // high
    w_up = up_weight[0]
    w_down = down_weight[0]

    vmem = pl.BlockSpec(memory_space=pltpu.VMEM)
    placer, placed_cells = pl.pallas_call(
        functools.partial(place_kernel, experts, low, high, capacity),
        out_shape=(
            jax.ShapeDtypeStruct((slot_count, all_rows), jnp.bfloat16),
            jax.ShapeDtypeStruct((slot_count, model_width), jnp.bfloat16),
        ),
        in_specs=[pl.BlockSpec(memory_space=pltpu.SMEM), vmem, vmem],
        out_specs=(vmem, vmem),
    )(me.astype(jnp.int32)[None], cluster_ids[:, :, 0], cell_rows.reshape(all_rows, model_width))
    placed_grads = jnp.dot(
        placer, cotangent.reshape(all_rows, model_width), preferred_element_type=jnp.float32
    ).astype(jnp.bfloat16)

    def send_near(placed):
        placed = placed.reshape(low, high, bucket, model_width)
        return jnp.stack(
            [placed[0]] + [swap(placed[step], step) for step in range(1, low)], axis=1
        )

    def send_far(near):
        far = [swap(near[step], step * low) for step in range(1, high)]
        return jnp.concatenate([piece.reshape(-1, model_width) for piece in far], axis=0)

    def copies(rows):
        pieces = []
        for shift in range(1, dp_count):
            ring = [(i, (i + shift) % dp_count) for i in range(dp_count)]
            pieces.append(lax.ppermute(rows, "dp", ring))
        return pieces

    def joined(first, second):
        return [jnp.concatenate(pair, axis=0) for pair in zip(first, second)]

    fence = lax.optimization_barrier

    def forward(features):
        pre_enc = jnp.dot(features, enc_weight, preferred_element_type=jnp.float32)
        silu_enc, slope_enc = silu_pair(pre_enc)
        encoded = features.astype(jnp.float32) + silu_enc
        inverse = lax.rsqrt(jnp.mean(encoded * encoded, axis=1, keepdims=True) + epsilon)
        norm_rows = (encoded * inverse).astype(jnp.bfloat16)
        pre_exp = jnp.dot(norm_rows, w_up, preferred_element_type=jnp.float32)
        silu_exp, slope_exp = silu_pair(pre_exp)
        return encoded, inverse, slope_enc, norm_rows, silu_exp.astype(jnp.bfloat16), slope_exp

    cells_near, placed_grads = fence((send_near(placed_cells), placed_grads))
    cells_here = cells_near[0].reshape(-1, model_width)
    cells_far, cells_here_copies, grads_near = fence(
        (send_far(cells_near), copies(cells_here), send_near(placed_grads))
    )
    grads_here = grads_near[0].reshape(-1, model_width)
    features = joined([cells_here], [cells_far])[0]
    grads_far, cells_far_copies, grads_here_copies, own_forward = fence(
        (send_far(grads_near), copies(cells_far), copies(grads_here), forward(features))
    )
    grads_far_copies = copies(grads_far)
    feature_parts = [features] + joined(cells_here_copies, cells_far_copies)
    forward_parts = [own_forward] + [forward(rows) for rows in feature_parts[1:]]
    grad_parts = joined([grads_here], [grads_far]) + joined(grads_here_copies, grads_far_copies)

    share = model_width // dp_count
    start = lax.axis_index("dp") * share
    block = share // experts

    def my_columns(rows):
        return lax.dynamic_slice_in_dim(rows, start, share, axis=1)

    stages = low.bit_length() - 1
    column = jnp.arange(share, dtype=jnp.int32)
    rank = column // block
    away = rank & (high - 1)
    away = away << stages
    for stage in range(stages):
        away = away | (((rank // high) >> (stages - 1 - stage)) & 1) << stage
    wanted = start + (away ^ me) * block + column % block
    picker = (jnp.arange(model_width, dtype=jnp.int32)[:, None] == wanted[None, :]).astype(
        jnp.bfloat16
    )

    norm_parts, pre_grad_parts, active_parts = [], [], []
    enc_parts = []
    for features, grad_rows, values in zip(feature_parts, grad_parts, forward_parts):
        encoded, inverse, slope_enc, norm_rows, active, slope_exp = values
        act_grad = jnp.dot(grad_rows, w_down, preferred_element_type=jnp.float32)
        pre_grad = (act_grad * slope_exp).astype(jnp.bfloat16)
        norm_grad = lax.dot_general(
            pre_grad, w_up, contract_last, preferred_element_type=jnp.float32
        )
        enc_rows_grad = inverse * norm_grad - inverse * inverse * inverse * encoded * jnp.mean(
            norm_grad * encoded, axis=1, keepdims=True
        )
        enc_pre_grad = (enc_rows_grad * slope_enc).astype(jnp.bfloat16)
        picked = jnp.dot(features, picker, preferred_element_type=jnp.float32).astype(jnp.bfloat16)
        enc_parts.append((picked, enc_pre_grad))
        norm_parts.append(my_columns(norm_rows))
        pre_grad_parts.append(pre_grad)
        active_parts.append(active)

    def enc_terms(first, last):
        total = None
        for picked, enc_pre_grad in enc_parts:
            term = lax.dot_general(
                picked[:, first:last],
                enc_pre_grad,
                contract_rows,
                preferred_element_type=jnp.float32,
            )
            total = term if total is None else total + term
        return total

    kept = share
    total = None
    for stage in range(stages):
        kept //= 2
        if total is None:
            sent, total = enc_terms(kept, 2 * kept), enc_terms(0, kept)
        else:
            sent, total = total[kept:], total[:kept]
        total = total + swap(sent.astype(jnp.bfloat16), 1 << stage).astype(jnp.float32)
    if total is None:
        total = enc_terms(0, share)
    sent = total.astype(jnp.bfloat16)
    total = total[:block]
    for step in range(1, high):
        piece = sent[step * block : (step + 1) * block]
        total = total + swap(piece, step * low).astype(jnp.float32)

    def rows_product(left, right):
        return lax.dot_general(
            jnp.concatenate(left, axis=0),
            jnp.concatenate(right, axis=0),
            contract_rows,
            preferred_element_type=jnp.float32,
        ).astype(jnp.bfloat16)

    up_sum = rows_product(norm_parts, pre_grad_parts)
    down_sum = rows_product([my_columns(g) for g in grad_parts], active_parts)
    return (total, up_sum[None], down_sum[None])


def solution(mesh):
    in_specs = (
        P(None, ("dp", "expert"), None),
        P(None, ("dp", "expert"), None),
        P(None, ("dp", "expert"), None),
        P(),
        P("expert", None, None),
        P("expert", None, None),
    )
    out_specs = (P(("dp", "expert"), None), P("expert", "dp", None), P("expert", "dp", None))
    return jax.shard_map(body, mesh=mesh, in_specs=in_specs, out_specs=out_specs, check_vma=False)
```

```python
import functools

import jax
import jax.numpy as jnp
from jax import lax
from jax.experimental import pallas as pl
from jax.experimental.pallas import tpu as pltpu
from jax.sharding import PartitionSpec as P

epsilon = 1e-06
contract_rows = (((0,), (0,)), ((), ()))
contract_last = (((1,), (1,)), ((), ()))


def silu_pair(pre_value):
    gate_value = jax.nn.sigmoid(pre_value)
    return (pre_value * gate_value, gate_value * (1.0 + pre_value * (1.0 - gate_value)))


def swap(piece, distance):
    pairs = [(i, i ^ distance) for i in range(lax.axis_size("expert"))]
    return lax.ppermute(piece, "expert", pairs)


def place_kernel(experts, low, high, capacity, me_ref, ids_ref, cells_ref, grads_ref, *refs):
    placed_refs, placer_ref = refs[:low], refs[low]
    batches, rows = ids_ref.shape
    width = cells_ref.shape[1]
    bucket = batches * capacity
    slots = experts * bucket
    earlier = (
        lax.broadcasted_iota(jnp.int32, (rows, rows), 0)
        < lax.broadcasted_iota(jnp.int32, (rows, rows), 1)
    )
    earlier = jnp.where(earlier, 1.0, 0.0).astype(jnp.bfloat16)
    for batch_index in range(batches):
        label = ids_ref[batch_index : batch_index + 1, :]
        named = lax.broadcasted_iota(jnp.int32, (experts, rows), 0) == label
        onehot = jnp.where(named, 1.0, 0.0)
        before = jnp.dot(onehot.astype(jnp.bfloat16), earlier, preferred_element_type=jnp.float32)
        rank = jnp.sum(before * onehot, axis=0, keepdims=True).astype(jnp.int32)
        away = label ^ me_ref[0]
        place = (away & (low - 1)) * high + (away >> (low.bit_length() - 1))
        slot = place * bucket + batch_index * capacity + rank
        hit = lax.broadcasted_iota(jnp.int32, (slots, rows), 0) == slot
        placer_ref[:, batch_index * rows : (batch_index + 1) * rows] = jnp.where(
            hit, 1.0, 0.0
        ).astype(jnp.bfloat16)
    piece = high * bucket
    for column, rows_ref in enumerate((cells_ref, grads_ref)):
        placed = jnp.dot(
            placer_ref[...], rows_ref[...], preferred_element_type=jnp.float32
        ).astype(jnp.bfloat16)
        for step in range(low):
            placed_refs[step][:, column * width : (column + 1) * width] = placed[
                step * piece : (step + 1) * piece
            ]


def body(cell_rows, cotangent, cluster_ids, enc_weight, up_weight, down_weight):
    experts = lax.axis_size("expert")
    dp_count = lax.axis_size("dp")
    me = lax.axis_index("expert")
    batch_count, local_rows, model_width = cell_rows.shape
    capacity = max(2, local_rows // 16)
    bucket = batch_count * capacity
    slot_count = experts * bucket
    all_rows = batch_count * local_rows
    high = min(4, experts)
    low = experts // high
    w_up = up_weight[0]
    w_down = down_weight[0]
    fence = lax.optimization_barrier

    vmem = pl.BlockSpec(memory_space=pltpu.VMEM)
    placed = pl.pallas_call(
        functools.partial(place_kernel, experts, low, high, capacity),
        out_shape=[jax.ShapeDtypeStruct((high * bucket, 2 * model_width), jnp.bfloat16)] * low,
        in_specs=[pl.BlockSpec(memory_space=pltpu.SMEM), vmem, vmem, vmem],
        out_specs=[vmem] * low,
        scratch_shapes=[pltpu.VMEM((slot_count, all_rows), jnp.bfloat16)],
    )(
        me.astype(jnp.int32)[None],
        cluster_ids[:, :, 0],
        cell_rows.reshape(all_rows, model_width),
        cotangent.reshape(all_rows, model_width),
    )

    def copies(rows):
        pieces = []
        for shift in range(1, dp_count):
            ring = [(i, (i + shift) % dp_count) for i in range(dp_count)]
            pieces.append(lax.ppermute(rows, "dp", ring))
        return pieces

    def forward(features):
        pre_enc = jnp.dot(features, enc_weight, preferred_element_type=jnp.float32)
        silu_enc, slope_enc = silu_pair(pre_enc)
        encoded = features.astype(jnp.float32) + silu_enc
        inverse = lax.rsqrt(jnp.mean(encoded * encoded, axis=1, keepdims=True) + epsilon)
        norm_rows = (encoded * inverse).astype(jnp.bfloat16)
        pre_exp = jnp.dot(norm_rows, w_up, preferred_element_type=jnp.float32)
        silu_exp, slope_exp = silu_pair(pre_exp)
        return encoded, inverse, slope_enc, norm_rows, silu_exp.astype(jnp.bfloat16), slope_exp

    near = [swap(placed[step], step) for step in range(1, low)]
    direct = [
        swap(placed[0][step * bucket : (step + 1) * bucket], step * low)
        for step in range(1, high)
    ]
    near, direct = fence((near, direct))
    early = [placed[0][:bucket]] + [piece[:bucket] for piece in near] + direct
    early = jnp.concatenate(early, axis=0)

    def send_far(first):
        far = []
        for step in range(1, high):
            pieces = [
                piece[step * bucket : (step + 1) * bucket, first : first + model_width]
                for piece in near
            ]
            far.append(swap(jnp.concatenate(pieces, axis=0), step * low))
        return far

    cells_far = send_far(0)
    grads_far = send_far(model_width)
    cells_far, early_copies = fence((cells_far, copies(early)))
    cells_far, early_copies = fence((jnp.concatenate(cells_far, axis=0), early_copies))

    def joined(first, second, column):
        return jnp.concatenate(
            [first[:, column * model_width : (column + 1) * model_width], second], axis=0
        )

    features = joined(early, cells_far, 0)
    grads_far, cells_far_copies, own_forward = fence(
        (grads_far, copies(cells_far), forward(features))
    )
    grads_far, cells_far_copies, own_forward = fence(
        (jnp.concatenate(grads_far, axis=0), cells_far_copies, own_forward)
    )
    grads_far_copies = copies(grads_far)
    feature_parts = [features] + [
        joined(*pair, 0) for pair in zip(early_copies, cells_far_copies)
    ]
    forward_parts = [own_forward] + [forward(rows) for rows in feature_parts[1:]]
    grad_parts = [joined(early, grads_far, 1)] + [
        joined(*pair, 1) for pair in zip(early_copies, grads_far_copies)
    ]

    share = model_width // dp_count
    start = lax.axis_index("dp") * share
    block = share // experts

    def my_columns(rows):
        return lax.dynamic_slice_in_dim(rows, start, share, axis=1)

    stages = low.bit_length() - 1
    column = jnp.arange(share, dtype=jnp.int32)
    rank = column // block
    away = rank & (high - 1)
    away = away << stages
    for stage in range(stages):
        away = away | (((rank // high) >> (stages - 1 - stage)) & 1) << stage
    wanted = start + (away ^ me) * block + column % block
    picker = (jnp.arange(model_width, dtype=jnp.int32)[:, None] == wanted[None, :]).astype(
        jnp.bfloat16
    )

    norm_parts, pre_grad_parts, active_parts = [], [], []
    enc_parts = []
    for features, grad_rows, values in zip(feature_parts, grad_parts, forward_parts):
        encoded, inverse, slope_enc, norm_rows, active, slope_exp = values
        act_grad = jnp.dot(grad_rows, w_down, preferred_element_type=jnp.float32)
        pre_grad = (act_grad * slope_exp).astype(jnp.bfloat16)
        norm_grad = lax.dot_general(
            pre_grad, w_up, contract_last, preferred_element_type=jnp.float32
        )
        enc_rows_grad = inverse * norm_grad - inverse * inverse * inverse * encoded * jnp.mean(
            norm_grad * encoded, axis=1, keepdims=True
        )
        enc_pre_grad = (enc_rows_grad * slope_enc).astype(jnp.bfloat16)
        picked = jnp.dot(features, picker, preferred_element_type=jnp.float32).astype(jnp.bfloat16)
        enc_parts.append((picked, enc_pre_grad))
        norm_parts.append(my_columns(norm_rows))
        pre_grad_parts.append(pre_grad)
        active_parts.append(active)

    def enc_terms(first, last):
        total = None
        for picked, enc_pre_grad in enc_parts:
            term = lax.dot_general(
                picked[:, first:last],
                enc_pre_grad,
                contract_rows,
                preferred_element_type=jnp.float32,
            )
            total = term if total is None else total + term
        return total

    kept = share
    total = None
    for stage in range(stages):
        kept //= 2
        if total is None:
            sent, total = enc_terms(kept, 2 * kept), enc_terms(0, kept)
        else:
            sent, total = total[kept:], total[:kept]
        total = total + swap(sent.astype(jnp.bfloat16), 1 << stage).astype(jnp.float32)
    if total is None:
        total = enc_terms(0, share)
    sent = total.astype(jnp.bfloat16)
    total = total[:block]
    for step in range(1, high):
        piece = sent[step * block : (step + 1) * block]
        total = total + swap(piece, step * low).astype(jnp.float32)

    def rows_product(left, right):
        return lax.dot_general(
            jnp.concatenate(left, axis=0),
            jnp.concatenate(right, axis=0),
            contract_rows,
            preferred_element_type=jnp.float32,
        ).astype(jnp.bfloat16)

    up_sum = rows_product(norm_parts, pre_grad_parts)
    down_sum = rows_product([my_columns(g) for g in grad_parts], active_parts)
    return (total, up_sum[None], down_sum[None])


def solution(mesh):
    in_specs = (
        P(None, ("dp", "expert"), None),
        P(None, ("dp", "expert"), None),
        P(None, ("dp", "expert"), None),
        P(),
        P("expert", None, None),
        P("expert", None, None),
    )
    out_specs = (P(("dp", "expert"), None), P("expert", "dp", None), P("expert", "dp", None))
    return jax.shard_map(body, mesh=mesh, in_specs=in_specs, out_specs=out_specs, check_vma=False)
```

```python
import functools

import jax
import jax.numpy as jnp
from jax import lax
from jax.experimental import pallas as pl
from jax.experimental.pallas import tpu as pltpu
from jax.sharding import PartitionSpec as P

epsilon = 1e-06
contract_rows = (((0,), (0,)), ((), ()))
contract_last = (((1,), (1,)), ((), ()))


def silu_pair(pre_value):
    gate_value = jax.nn.sigmoid(pre_value)
    return (pre_value * gate_value, gate_value * (1.0 + pre_value * (1.0 - gate_value)))


def swap(piece, distance):
    pairs = [(i, i ^ distance) for i in range(lax.axis_size("expert"))]
    return lax.ppermute(piece, "expert", pairs)


def place_kernel(experts, low, high, capacity, me_ref, ids_ref, *refs):
    rows_refs, here_refs, refs = refs[:2], refs[2:4], refs[4:]
    near_refs, direct_refs, placer_ref = refs[: 2 * (low - 1)], refs[2 * (low - 1) : -1], refs[-1]
    batches, rows = ids_ref.shape
    bucket = batches * capacity
    piece = high * bucket
    slots = experts * bucket
    earlier = (
        lax.broadcasted_iota(jnp.int32, (rows, rows), 0)
        < lax.broadcasted_iota(jnp.int32, (rows, rows), 1)
    )
    earlier = jnp.where(earlier, 1.0, 0.0).astype(jnp.bfloat16)
    for batch_index in range(batches):
        label = ids_ref[batch_index : batch_index + 1, :]
        named = lax.broadcasted_iota(jnp.int32, (experts, rows), 0) == label
        onehot = jnp.where(named, 1.0, 0.0)
        before = jnp.dot(onehot.astype(jnp.bfloat16), earlier, preferred_element_type=jnp.float32)
        rank = jnp.sum(before * onehot, axis=0, keepdims=True).astype(jnp.int32)
        away = label ^ me_ref[0]
        place = (away & (low - 1)) * high + (away >> (low.bit_length() - 1))
        slot = place * bucket + batch_index * capacity + rank
        hit = lax.broadcasted_iota(jnp.int32, (slots, rows), 0) == slot
        placer_ref[:, batch_index * rows : (batch_index + 1) * rows] = jnp.where(
            hit, 1.0, 0.0
        ).astype(jnp.bfloat16)
    for kind in range(2):
        placed = jnp.dot(
            placer_ref[...], rows_refs[kind][...], preferred_element_type=jnp.float32
        ).astype(jnp.bfloat16)
        here_refs[kind][...] = placed[:bucket]
        for step in range(1, high):
            direct_refs[step - 1][kind * bucket : (kind + 1) * bucket] = placed[
                step * bucket : (step + 1) * bucket
            ]
        for step in range(1, low):
            near_refs[kind * (low - 1) + step - 1][...] = placed[
                step * piece : (step + 1) * piece
            ]


def body(cell_rows, cotangent, cluster_ids, enc_weight, up_weight, down_weight):
    experts = lax.axis_size("expert")
    dp_count = lax.axis_size("dp")
    me = lax.axis_index("expert")
    batch_count, local_rows, model_width = cell_rows.shape
    capacity = max(2, local_rows // 16)
    bucket = batch_count * capacity
    slot_count = experts * bucket
    all_rows = batch_count * local_rows
    high = min(4, experts)
    low = experts // high
    w_up = up_weight[0]
    w_down = down_weight[0]
    fence = lax.optimization_barrier

    vmem = pl.BlockSpec(memory_space=pltpu.VMEM)
    heights = [bucket] * 2 + [high * bucket] * (2 * (low - 1)) + [2 * bucket] * (high - 1)
    placed = pl.pallas_call(
        functools.partial(place_kernel, experts, low, high, capacity),
        out_shape=[jax.ShapeDtypeStruct((rows, model_width), jnp.bfloat16) for rows in heights],
        in_specs=[pl.BlockSpec(memory_space=pltpu.SMEM), vmem, vmem, vmem],
        out_specs=[vmem] * len(heights),
        scratch_shapes=[pltpu.VMEM((slot_count, all_rows), jnp.bfloat16)],
    )(
        me.astype(jnp.int32)[None],
        cluster_ids[:, :, 0],
        cell_rows.reshape(all_rows, model_width),
        cotangent.reshape(all_rows, model_width),
    )
    here, placed = placed[:2], placed[2:]
    cells_placed, grads_placed = placed[: low - 1], placed[low - 1 : 2 * (low - 1)]
    direct_placed = placed[2 * (low - 1) :]

    def copies(rows):
        pieces = []
        for shift in range(1, dp_count):
            ring = [(i, (i + shift) % dp_count) for i in range(dp_count)]
            pieces.append(lax.ppermute(rows, "dp", ring))
        return pieces

    def forward(features):
        pre_enc = jnp.dot(features, enc_weight, preferred_element_type=jnp.float32)
        silu_enc, slope_enc = silu_pair(pre_enc)
        encoded = features.astype(jnp.float32) + silu_enc
        inverse = lax.rsqrt(jnp.mean(encoded * encoded, axis=1, keepdims=True) + epsilon)
        norm_rows = (encoded * inverse).astype(jnp.bfloat16)
        pre_exp = jnp.dot(norm_rows, w_up, preferred_element_type=jnp.float32)
        silu_exp, slope_exp = silu_pair(pre_exp)
        return encoded, inverse, slope_enc, norm_rows, silu_exp.astype(jnp.bfloat16), slope_exp

    def stack(*pieces):
        return jnp.concatenate(pieces, axis=0)

    def send_near(pieces):
        return [swap(pieces[step - 1], step) for step in range(low - 1, 0, -1)]

    def far_pieces(near):
        return [
            stack(*[piece[step * bucket : (step + 1) * bucket] for piece in near])
            for step in range(high - 1, 0, -1)
        ]

    def send_far(pieces):
        return [swap(piece, step * low) for piece, step in zip(pieces, range(high - 1, 0, -1))]

    def here_and_near(own, near):
        return stack(own, *[piece[:bucket] for piece in near])

    cells_near = send_near(cells_placed)
    direct = [swap(direct_placed[step - 1], step * low) for step in range(high - 1, 0, -1)]
    cells_near, direct, here, grads_placed = fence((cells_near, direct, here, grads_placed))
    cells_early = stack(here_and_near(here[0], cells_near), *[both[:bucket] for both in direct])
    grads_direct = stack(*[both[bucket:] for both in direct])
    early_rows = cells_early.shape[0]
    early, cells_far, grads_placed = fence(
        (stack(cells_early, grads_direct), far_pieces(cells_near), grads_placed)
    )
    early_copies = copies(early)
    cells_far = send_far(cells_far)
    grads_near = send_near(grads_placed)
    grads_far = send_far(far_pieces(grads_near))
    cells_far, early_copies, grads_near = fence((cells_far, early_copies, grads_near))
    cells_far = stack(*cells_far)
    grads_near = here_and_near(here[1], grads_near)
    far_rows = cells_far.shape[0]
    cells_far, grads_near, early_copies = fence((cells_far, grads_near, early_copies))
    middle_copies = copies(stack(cells_far, grads_near))
    features = stack(cells_early, cells_far)
    grads_far, middle_copies, own_forward = fence((grads_far, middle_copies, forward(features)))
    grads_far, middle_copies, own_forward = fence(
        (stack(*grads_far), middle_copies, own_forward)
    )
    last_copies = copies(grads_far)
    feature_parts = [features] + [
        stack(early[:early_rows], middle[:far_rows])
        for early, middle in zip(early_copies, middle_copies)
    ]
    grad_parts = [stack(grads_near, grads_direct, grads_far)] + [
        stack(middle[far_rows:], early[early_rows:], last)
        for early, middle, last in zip(early_copies, middle_copies, last_copies)
    ]
    forward_parts = [own_forward] + [forward(rows) for rows in feature_parts[1:]]

    share = model_width // dp_count
    start = lax.axis_index("dp") * share
    block = share // experts

    def my_columns(rows):
        return lax.dynamic_slice_in_dim(rows, start, share, axis=1)

    stages = low.bit_length() - 1
    column = jnp.arange(share, dtype=jnp.int32)
    rank = column // block
    away = rank & (high - 1)
    away = away << stages
    for stage in range(stages):
        away = away | (((rank // high) >> (stages - 1 - stage)) & 1) << stage
    wanted = start + (away ^ me) * block + column % block
    picker = (jnp.arange(model_width, dtype=jnp.int32)[:, None] == wanted[None, :]).astype(
        jnp.bfloat16
    )

    norm_parts, pre_grad_parts, active_parts = [], [], []
    enc_parts = []
    for features, grad_rows, values in zip(feature_parts, grad_parts, forward_parts):
        encoded, inverse, slope_enc, norm_rows, active, slope_exp = values
        act_grad = jnp.dot(grad_rows, w_down, preferred_element_type=jnp.float32)
        pre_grad = (act_grad * slope_exp).astype(jnp.bfloat16)
        norm_grad = lax.dot_general(
            pre_grad, w_up, contract_last, preferred_element_type=jnp.float32
        )
        enc_rows_grad = inverse * norm_grad - inverse * inverse * inverse * encoded * jnp.mean(
            norm_grad * encoded, axis=1, keepdims=True
        )
        enc_pre_grad = (enc_rows_grad * slope_enc).astype(jnp.bfloat16)
        picked = jnp.dot(features, picker, preferred_element_type=jnp.float32).astype(jnp.bfloat16)
        enc_parts.append((picked, enc_pre_grad))
        norm_parts.append(my_columns(norm_rows))
        pre_grad_parts.append(pre_grad)
        active_parts.append(active)

    def enc_terms(first, last):
        total = None
        for picked, enc_pre_grad in enc_parts:
            term = lax.dot_general(
                picked[:, first:last],
                enc_pre_grad,
                contract_rows,
                preferred_element_type=jnp.float32,
            )
            total = term if total is None else total + term
        return total

    kept = share
    total = None
    for stage in range(stages):
        kept //= 2
        if total is None:
            sent, total = enc_terms(kept, 2 * kept), enc_terms(0, kept)
        else:
            sent, total = total[kept:], total[:kept]
        total = total + swap(sent.astype(jnp.bfloat16), 1 << stage).astype(jnp.float32)
    if total is None:
        total = enc_terms(0, share)
    sent = total.astype(jnp.bfloat16)
    total = total[:block]
    for step in range(1, high):
        piece = sent[step * block : (step + 1) * block]
        total = total + swap(piece, step * low).astype(jnp.float32)

    def rows_product(left, right):
        return lax.dot_general(
            jnp.concatenate(left, axis=0),
            jnp.concatenate(right, axis=0),
            contract_rows,
            preferred_element_type=jnp.float32,
        ).astype(jnp.bfloat16)

    up_sum = rows_product(norm_parts, pre_grad_parts)
    down_sum = rows_product([my_columns(g) for g in grad_parts], active_parts)
    return (total, up_sum[None], down_sum[None])


def solution(mesh):
    in_specs = (
        P(None, ("dp", "expert"), None),
        P(None, ("dp", "expert"), None),
        P(None, ("dp", "expert"), None),
        P(),
        P("expert", None, None),
        P("expert", None, None),
    )
    out_specs = (P(("dp", "expert"), None), P("expert", "dp", None), P("expert", "dp", None))
    return jax.shard_map(body, mesh=mesh, in_specs=in_specs, out_specs=out_specs, check_vma=False)
```

```python
import functools

import jax
import jax.numpy as jnp
from jax import lax
from jax.experimental import pallas as pl
from jax.experimental.pallas import tpu as pltpu
from jax.sharding import PartitionSpec as P

epsilon = 1e-06
contract_rows = (((0,), (0,)), ((), ()))
contract_last = (((1,), (1,)), ((), ()))


def silu_pair(pre_value):
    gate_value = jax.nn.sigmoid(pre_value)
    return (pre_value * gate_value, gate_value * (1.0 + pre_value * (1.0 - gate_value)))


def swap(piece, distance):
    pairs = [(i, i ^ distance) for i in range(lax.axis_size("expert"))]
    return lax.ppermute(piece, "expert", pairs)


def place_kernel(experts, low, high, capacity, me_ref, ids_ref, *refs):
    rows_refs, here_refs, refs = refs[:2], refs[2:4], refs[4:]
    near_refs, direct_refs, placer_ref = refs[: 2 * (low - 1)], refs[2 * (low - 1) : -1], refs[-1]
    batches, rows = ids_ref.shape
    bucket = batches * capacity
    piece = high * bucket
    slots = experts * bucket
    earlier = (
        lax.broadcasted_iota(jnp.int32, (rows, rows), 0)
        < lax.broadcasted_iota(jnp.int32, (rows, rows), 1)
    )
    earlier = jnp.where(earlier, 1.0, 0.0).astype(jnp.bfloat16)
    for batch_index in range(batches):
        label = ids_ref[batch_index : batch_index + 1, :]
        named = lax.broadcasted_iota(jnp.int32, (experts, rows), 0) == label
        onehot = jnp.where(named, 1.0, 0.0)
        before = jnp.dot(onehot.astype(jnp.bfloat16), earlier, preferred_element_type=jnp.float32)
        rank = jnp.sum(before * onehot, axis=0, keepdims=True).astype(jnp.int32)
        away = label ^ me_ref[0]
        place = (away & (low - 1)) * high + (away >> (low.bit_length() - 1))
        slot = place * bucket + batch_index * capacity + rank
        hit = lax.broadcasted_iota(jnp.int32, (slots, rows), 0) == slot
        placer_ref[:, batch_index * rows : (batch_index + 1) * rows] = jnp.where(
            hit, 1.0, 0.0
        ).astype(jnp.bfloat16)
    for kind in range(2):
        placed = jnp.dot(
            placer_ref[...], rows_refs[kind][...], preferred_element_type=jnp.float32
        ).astype(jnp.bfloat16)
        here_refs[kind][...] = placed[:bucket]
        for step in range(1, high):
            direct_refs[step - 1][kind * bucket : (kind + 1) * bucket] = placed[
                step * bucket : (step + 1) * bucket
            ]
        for step in range(1, low):
            near_refs[kind * (low - 1) + step - 1][...] = placed[
                step * piece : (step + 1) * piece
            ]


def pack_kernel(bucket, high, *refs):
    here_ref, refs, outs = refs[0], refs[1:-high], refs[-high:]
    near_refs, direct_refs = refs[: -(high - 1)], refs[-(high - 1) :]
    early_ref, far_refs = outs[0], outs[1:]
    early_ref[:bucket] = here_ref[...]
    at = bucket
    for near_ref in near_refs:
        early_ref[at : at + bucket] = near_ref[:bucket]
        at += bucket
    for kind in range(2):
        for direct_ref in direct_refs:
            early_ref[at : at + bucket] = direct_ref[kind * bucket : (kind + 1) * bucket]
            at += bucket
    for index, far_ref in enumerate(far_refs):
        step = high - 1 - index
        for place, near_ref in enumerate(near_refs):
            far_ref[place * bucket : (place + 1) * bucket] = near_ref[
                step * bucket : (step + 1) * bucket
            ]


def body(cell_rows, cotangent, cluster_ids, enc_weight, up_weight, down_weight):
    experts = lax.axis_size("expert")
    dp_count = lax.axis_size("dp")
    me = lax.axis_index("expert")
    batch_count, local_rows, model_width = cell_rows.shape
    capacity = max(2, local_rows // 16)
    bucket = batch_count * capacity
    slot_count = experts * bucket
    all_rows = batch_count * local_rows
    high = min(4, experts)
    low = experts // high
    w_up = up_weight[0]
    w_down = down_weight[0]
    fence = lax.optimization_barrier

    vmem = pl.BlockSpec(memory_space=pltpu.VMEM)
    heights = [bucket] * 2 + [high * bucket] * (2 * (low - 1)) + [2 * bucket] * (high - 1)
    placed = pl.pallas_call(
        functools.partial(place_kernel, experts, low, high, capacity),
        out_shape=[jax.ShapeDtypeStruct((rows, model_width), jnp.bfloat16) for rows in heights],
        in_specs=[pl.BlockSpec(memory_space=pltpu.SMEM), vmem, vmem, vmem],
        out_specs=[vmem] * len(heights),
        scratch_shapes=[pltpu.VMEM((slot_count, all_rows), jnp.bfloat16)],
    )(
        me.astype(jnp.int32)[None],
        cluster_ids[:, :, 0],
        cell_rows.reshape(all_rows, model_width),
        cotangent.reshape(all_rows, model_width),
    )
    here, placed = placed[:2], placed[2:]
    cells_placed, grads_placed = placed[: low - 1], placed[low - 1 : 2 * (low - 1)]
    direct_placed = placed[2 * (low - 1) :]

    def copies(rows):
        pieces = []
        for shift in range(1, dp_count):
            ring = [(i, (i + shift) % dp_count) for i in range(dp_count)]
            pieces.append(lax.ppermute(rows, "dp", ring))
        return pieces

    def forward(features):
        pre_enc = jnp.dot(features, enc_weight, preferred_element_type=jnp.float32)
        silu_enc, slope_enc = silu_pair(pre_enc)
        encoded = features.astype(jnp.float32) + silu_enc
        inverse = lax.rsqrt(jnp.mean(encoded * encoded, axis=1, keepdims=True) + epsilon)
        norm_rows = (encoded * inverse).astype(jnp.bfloat16)
        pre_exp = jnp.dot(norm_rows, w_up, preferred_element_type=jnp.float32)
        silu_exp, slope_exp = silu_pair(pre_exp)
        return encoded, inverse, slope_enc, norm_rows, silu_exp.astype(jnp.bfloat16), slope_exp

    def stack(*pieces):
        return jnp.concatenate(pieces, axis=0)

    def send_near(pieces):
        return [swap(pieces[step - 1], step) for step in range(low - 1, 0, -1)]

    def far_pieces(near):
        return [
            stack(*[piece[step * bucket : (step + 1) * bucket] for piece in near])
            for step in range(high - 1, 0, -1)
        ]

    def send_far(pieces):
        return [swap(piece, step * low) for piece, step in zip(pieces, range(high - 1, 0, -1))]

    def here_and_near(own, near):
        return stack(own, *[piece[:bucket] for piece in near])

    cells_near = send_near(cells_placed)
    direct_placed, cells_near[-1] = fence((direct_placed, cells_near[-1]))
    direct = [swap(direct_placed[step - 1], step * low) for step in range(high - 1, 0, -1)]
    cells_near, direct, here, grads_placed = fence((cells_near, direct, here, grads_placed))
    early_rows = (low + high - 1) * bucket
    heights = [early_rows + (high - 1) * bucket] + [(low - 1) * bucket] * (high - 1)
    early, *cells_far = pl.pallas_call(
        functools.partial(pack_kernel, bucket, high),
        out_shape=[jax.ShapeDtypeStruct((rows, model_width), jnp.bfloat16) for rows in heights],
        in_specs=[vmem] * (1 + len(cells_near) + len(direct)),
        out_specs=[vmem] * len(heights),
    )(here[0], *cells_near, *direct)
    cells_early, grads_direct = early[:early_rows], early[early_rows:]
    early_copies = copies(early)
    cells_far = send_far(cells_far)
    grads_near = send_near(grads_placed)
    grads_near, early_copies = fence((grads_near, early_copies))
    grads_far = send_far(far_pieces(grads_near))
    cells_far = fence(cells_far)
    cells_far, grads_near, early_copies = fence(
        (stack(*cells_far), here_and_near(here[1], grads_near), early_copies)
    )
    far_rows = cells_far.shape[0]
    middle_copies = copies(stack(cells_far, grads_near))
    features = stack(cells_early, cells_far)
    grads_far, own_forward = fence((grads_far, forward(features)))
    grads_far, own_forward = fence((stack(*grads_far), own_forward))
    last_copies = copies(grads_far)

    share = model_width // dp_count
    start = lax.axis_index("dp") * share
    block = share // experts

    def my_columns(rows):
        return lax.dynamic_slice_in_dim(rows, start, share, axis=1)

    stages = low.bit_length() - 1
    column = jnp.arange(share, dtype=jnp.int32)
    rank = column // block
    away = rank & (high - 1)
    away = away << stages
    for stage in range(stages):
        away = away | (((rank // high) >> (stages - 1 - stage)) & 1) << stage
    wanted = start + (away ^ me) * block + column % block
    picker = (jnp.arange(model_width, dtype=jnp.int32)[:, None] == wanted[None, :]).astype(
        jnp.bfloat16
    )

    norm_parts, pre_grad_parts, active_parts, grad_parts = [], [], [], []
    enc_parts = []

    def backward(features, grad_rows, values):
        encoded, inverse, slope_enc, norm_rows, active, slope_exp = values
        act_grad = jnp.dot(grad_rows, w_down, preferred_element_type=jnp.float32)
        pre_grad = (act_grad * slope_exp).astype(jnp.bfloat16)
        norm_grad = lax.dot_general(
            pre_grad, w_up, contract_last, preferred_element_type=jnp.float32
        )
        enc_rows_grad = inverse * norm_grad - inverse * inverse * inverse * encoded * jnp.mean(
            norm_grad * encoded, axis=1, keepdims=True
        )
        enc_pre_grad = (enc_rows_grad * slope_enc).astype(jnp.bfloat16)
        picked = jnp.dot(features, picker, preferred_element_type=jnp.float32).astype(jnp.bfloat16)
        enc_parts.append((picked, enc_pre_grad))
        norm_parts.append(my_columns(norm_rows))
        pre_grad_parts.append(pre_grad)
        active_parts.append(active)
        grad_parts.append(my_columns(grad_rows))

    backward(features, stack(grads_near, grads_direct, grads_far), own_forward)
    middle_copies, enc_parts[0] = fence((middle_copies, enc_parts[0]))
    for early, middle, last in zip(early_copies, middle_copies, last_copies):
        features = stack(early[:early_rows], middle[:far_rows])
        grad_rows = stack(middle[far_rows:], early[early_rows:], last)
        backward(features, grad_rows, forward(features))

    def enc_terms(first, last):
        total = None
        for picked, enc_pre_grad in enc_parts:
            term = lax.dot_general(
                picked[:, first:last],
                enc_pre_grad,
                contract_rows,
                preferred_element_type=jnp.float32,
            )
            total = term if total is None else total + term
        return total

    kept = share
    total = None
    for stage in range(stages):
        kept //= 2
        if total is None:
            sent, total = enc_terms(kept, 2 * kept), enc_terms(0, kept)
        else:
            sent, total = total[kept:], total[:kept]
        total = total + swap(sent.astype(jnp.bfloat16), 1 << stage).astype(jnp.float32)
    if total is None:
        total = enc_terms(0, share)
    sent = total.astype(jnp.bfloat16)
    total = total[:block]
    for step in range(1, high):
        piece = sent[step * block : (step + 1) * block]
        total = total + swap(piece, step * low).astype(jnp.float32)

    def rows_product(left, right):
        return lax.dot_general(
            jnp.concatenate(left, axis=0),
            jnp.concatenate(right, axis=0),
            contract_rows,
            preferred_element_type=jnp.float32,
        ).astype(jnp.bfloat16)

    up_sum = rows_product(norm_parts, pre_grad_parts)
    down_sum = rows_product(grad_parts, active_parts)
    return (total, up_sum[None], down_sum[None])


def solution(mesh):
    in_specs = (
        P(None, ("dp", "expert"), None),
        P(None, ("dp", "expert"), None),
        P(None, ("dp", "expert"), None),
        P(),
        P("expert", None, None),
        P("expert", None, None),
    )
    out_specs = (P(("dp", "expert"), None), P("expert", "dp", None), P("expert", "dp", None))
    return jax.shard_map(body, mesh=mesh, in_specs=in_specs, out_specs=out_specs, check_vma=False)
```

```python
import functools

import jax
import jax.numpy as jnp
from jax import lax
from jax.experimental import pallas as pl
from jax.experimental.pallas import tpu as pltpu
from jax.sharding import PartitionSpec as P

epsilon = 1e-06
contract_rows = (((0,), (0,)), ((), ()))
contract_last = (((1,), (1,)), ((), ()))


def silu_pair(pre_value):
    gate_value = jax.nn.sigmoid(pre_value)
    return (pre_value * gate_value, gate_value * (1.0 + pre_value * (1.0 - gate_value)))


def swap(piece, distance):
    pairs = [(i, i ^ distance) for i in range(lax.axis_size("expert"))]
    return lax.ppermute(piece, "expert", pairs)


def place_kernel(experts, low, high, capacity, me_ref, ids_ref, *refs):
    rows_refs, here_refs, refs = refs[:2], refs[2:4], refs[4:]
    near_refs, direct_refs, placer_ref = refs[: 2 * (low - 1)], refs[2 * (low - 1) : -1], refs[-1]
    batches, rows = ids_ref.shape
    width = rows_refs[0].shape[1]
    bucket = batches * capacity
    piece = high * bucket
    slots = experts * bucket
    earlier = (
        lax.broadcasted_iota(jnp.int32, (rows, rows), 0)
        < lax.broadcasted_iota(jnp.int32, (rows, rows), 1)
    )
    earlier = jnp.where(earlier, 1.0, 0.0).astype(jnp.bfloat16)
    for batch_index in range(batches):
        label = ids_ref[batch_index : batch_index + 1, :]
        named = lax.broadcasted_iota(jnp.int32, (experts, rows), 0) == label
        onehot = jnp.where(named, 1.0, 0.0)
        before = jnp.dot(onehot.astype(jnp.bfloat16), earlier, preferred_element_type=jnp.float32)
        rank = jnp.sum(before * onehot, axis=0, keepdims=True).astype(jnp.int32)
        away = label ^ me_ref[0]
        place = (away & (low - 1)) * high + (away >> (low.bit_length() - 1))
        slot = place * bucket + batch_index * capacity + rank
        hit = lax.broadcasted_iota(jnp.int32, (slots, rows), 0) == slot
        placer_ref[:, batch_index * rows : (batch_index + 1) * rows] = jnp.where(
            hit, 1.0, 0.0
        ).astype(jnp.bfloat16)
    for kind in range(2):
        placed = jnp.dot(
            placer_ref[...], rows_refs[kind][...], preferred_element_type=jnp.float32
        ).astype(jnp.bfloat16)
        here_refs[kind][...] = placed[:bucket]
        for step in range(1, high):
            direct_refs[step - 1][:, kind * width : (kind + 1) * width] = placed[
                step * bucket : (step + 1) * bucket
            ]
        for step in range(1, low):
            near_refs[kind * (low - 1) + step - 1][...] = placed[
                step * piece : (step + 1) * piece
            ]


def body(cell_rows, cotangent, cluster_ids, enc_weight, up_weight, down_weight):
    experts = lax.axis_size("expert")
    dp_count = lax.axis_size("dp")
    me = lax.axis_index("expert")
    batch_count, local_rows, model_width = cell_rows.shape
    capacity = max(2, local_rows // 16)
    bucket = batch_count * capacity
    slot_count = experts * bucket
    all_rows = batch_count * local_rows
    high = min(4, experts)
    low = experts // high
    w_up = up_weight[0]
    w_down = down_weight[0]
    fence = lax.optimization_barrier

    vmem = pl.BlockSpec(memory_space=pltpu.VMEM)
    shapes = [(bucket, model_width)] * 2 + [(high * bucket, model_width)] * (2 * (low - 1))
    shapes += [(bucket, 2 * model_width)] * (high - 1)
    placed = pl.pallas_call(
        functools.partial(place_kernel, experts, low, high, capacity),
        out_shape=[jax.ShapeDtypeStruct(shape, jnp.bfloat16) for shape in shapes],
        in_specs=[pl.BlockSpec(memory_space=pltpu.SMEM), vmem, vmem, vmem],
        out_specs=[vmem] * len(shapes),
        scratch_shapes=[pltpu.VMEM((slot_count, all_rows), jnp.bfloat16)],
    )(
        me.astype(jnp.int32)[None],
        cluster_ids[:, :, 0],
        cell_rows.reshape(all_rows, model_width),
        cotangent.reshape(all_rows, model_width),
    )
    here, placed = placed[:2], placed[2:]
    cells_placed, grads_placed = placed[: low - 1], placed[low - 1 : 2 * (low - 1)]
    direct_placed = placed[2 * (low - 1) :]

    def copies(rows):
        pieces = []
        for shift in range(1, dp_count):
            ring = [(i, (i + shift) % dp_count) for i in range(dp_count)]
            pieces.append(lax.ppermute(rows, "dp", ring))
        return pieces

    def forward(features):
        pre_enc = jnp.dot(features, enc_weight, preferred_element_type=jnp.float32)
        silu_enc, slope_enc = silu_pair(pre_enc)
        encoded = features.astype(jnp.float32) + silu_enc
        inverse = lax.rsqrt(jnp.mean(encoded * encoded, axis=1, keepdims=True) + epsilon)
        norm_rows = (encoded * inverse).astype(jnp.bfloat16)
        pre_exp = jnp.dot(norm_rows, w_up, preferred_element_type=jnp.float32)
        silu_exp, slope_exp = silu_pair(pre_exp)
        return encoded, inverse, slope_enc, norm_rows, silu_exp.astype(jnp.bfloat16), slope_exp

    def stack(*pieces):
        return jnp.concatenate(pieces, axis=0)

    def send_near(pieces):
        return [swap(pieces[step - 1], step) for step in range(low - 1, 0, -1)]

    def far_pieces(near):
        return [
            stack(*[piece[step * bucket : (step + 1) * bucket] for piece in near])
            for step in range(high - 1, 0, -1)
        ]

    def send_far(pieces):
        return [swap(piece, step * low) for piece, step in zip(pieces, range(high - 1, 0, -1))]

    def here_and_near(own, near):
        return stack(own, *[piece[:bucket] for piece in near])

    cells_near = send_near(cells_placed)
    direct_placed, cells_near[-1] = fence((direct_placed, cells_near[-1]))
    direct = [swap(direct_placed[step - 1], step * low) for step in range(high - 1, 0, -1)]
    cells_near, direct, here, grads_placed = fence((cells_near, direct, here, grads_placed))
    cells_first, direct, cells_far, grads_placed = fence(
        (
            here_and_near(here[0], cells_near),
            stack(*direct),
            far_pieces(cells_near),
            grads_placed,
        )
    )
    cells_first_copies = copies(cells_first)
    grads_near = send_near(grads_placed)
    cells_far = send_far(cells_far)
    direct_copies = copies(direct)
    grads_near, cells_first_copies = fence((grads_near, cells_first_copies))
    grads_first = here_and_near(here[1], grads_near)
    grads_first_copies = copies(grads_first)
    grads_far = send_far(far_pieces(grads_near))
    came = (cells_first_copies, direct_copies, grads_first_copies)
    cells_far, came = fence((cells_far, came))
    cells_far, came = fence((stack(*cells_far), came))
    cells_far_copies = copies(cells_far)
    features = stack(cells_first, direct[:, :model_width], cells_far)
    grads_far, own_forward = fence((grads_far, forward(features)))
    grads_far, own_forward = fence((stack(*grads_far), own_forward))
    grads_far_copies = copies(grads_far)

    share = model_width // dp_count
    start = lax.axis_index("dp") * share
    block = share // experts

    def my_columns(rows):
        return lax.dynamic_slice_in_dim(rows, start, share, axis=1)

    stages = low.bit_length() - 1
    column = jnp.arange(share, dtype=jnp.int32)
    rank = column // block
    away = rank & (high - 1)
    away = away << stages
    for stage in range(stages):
        away = away | (((rank // high) >> (stages - 1 - stage)) & 1) << stage
    wanted = start + (away ^ me) * block + column % block
    picker = (jnp.arange(model_width, dtype=jnp.int32)[:, None] == wanted[None, :]).astype(
        jnp.bfloat16
    )

    norm_parts, pre_grad_parts, active_parts, grad_parts = [], [], [], []
    enc_parts = []

    def backward(features, grad_rows, values):
        encoded, inverse, slope_enc, norm_rows, active, slope_exp = values
        act_grad = jnp.dot(grad_rows, w_down, preferred_element_type=jnp.float32)
        pre_grad = (act_grad * slope_exp).astype(jnp.bfloat16)
        norm_grad = lax.dot_general(
            pre_grad, w_up, contract_last, preferred_element_type=jnp.float32
        )
        enc_rows_grad = inverse * norm_grad - inverse * inverse * inverse * encoded * jnp.mean(
            norm_grad * encoded, axis=1, keepdims=True
        )
        enc_pre_grad = (enc_rows_grad * slope_enc).astype(jnp.bfloat16)
        picked = jnp.dot(features, picker, preferred_element_type=jnp.float32).astype(jnp.bfloat16)
        enc_parts.append((picked, enc_pre_grad))
        norm_parts.append(my_columns(norm_rows))
        pre_grad_parts.append(pre_grad)
        active_parts.append(active)
        grad_parts.append(my_columns(grad_rows))

    backward(features, stack(grads_first, direct[:, model_width:], grads_far), own_forward)
    cells_far_copies, enc_parts[0] = fence((cells_far_copies, enc_parts[0]))
    for cells_first, direct, grads_first, cells_far, grads_far in zip(
        *came, cells_far_copies, grads_far_copies
    ):
        features = stack(cells_first, direct[:, :model_width], cells_far)
        grad_rows = stack(grads_first, direct[:, model_width:], grads_far)
        backward(features, grad_rows, forward(features))

    def enc_terms(first, last):
        total = None
        for picked, enc_pre_grad in enc_parts:
            term = lax.dot_general(
                picked[:, first:last],
                enc_pre_grad,
                contract_rows,
                preferred_element_type=jnp.float32,
            )
            total = term if total is None else total + term
        return total

    kept = share
    total = None
    for stage in range(stages):
        kept //= 2
        if total is None:
            sent, total = enc_terms(kept, 2 * kept), enc_terms(0, kept)
        else:
            sent, total = total[kept:], total[:kept]
        total = total + swap(sent.astype(jnp.bfloat16), 1 << stage).astype(jnp.float32)
    if total is None:
        total = enc_terms(0, share)
    sent = total.astype(jnp.bfloat16)
    total = total[:block]
    for step in range(1, high):
        piece = sent[step * block : (step + 1) * block]
        total = total + swap(piece, step * low).astype(jnp.float32)

    def rows_product(left, right):
        return lax.dot_general(
            jnp.concatenate(left, axis=0),
            jnp.concatenate(right, axis=0),
            contract_rows,
            preferred_element_type=jnp.float32,
        ).astype(jnp.bfloat16)

    up_sum = rows_product(norm_parts, pre_grad_parts)
    down_sum = rows_product(grad_parts, active_parts)
    return (total, up_sum[None], down_sum[None])


def solution(mesh):
    in_specs = (
        P(None, ("dp", "expert"), None),
        P(None, ("dp", "expert"), None),
        P(None, ("dp", "expert"), None),
        P(),
        P("expert", None, None),
        P("expert", None, None),
    )
    out_specs = (P(("dp", "expert"), None), P("expert", "dp", None), P("expert", "dp", None))
    return jax.shard_map(body, mesh=mesh, in_specs=in_specs, out_specs=out_specs, check_vma=False)
```

```python
import functools

import jax
import jax.numpy as jnp
from jax import lax
from jax.experimental import pallas as pl
from jax.experimental.pallas import tpu as pltpu
from jax.sharding import PartitionSpec as P

epsilon = 1e-06
contract_rows = (((0,), (0,)), ((), ()))
contract_last = (((1,), (1,)), ((), ()))


def silu_pair(pre_value):
    gate_value = jax.nn.sigmoid(pre_value)
    return (pre_value * gate_value, gate_value * (1.0 + pre_value * (1.0 - gate_value)))


def swap(piece, distance):
    pairs = [(i, i ^ distance) for i in range(lax.axis_size("expert"))]
    return lax.ppermute(piece, "expert", pairs)


def place_kernel(experts, low, high, capacity, direct_steps, me_ref, ids_ref, *refs):
    rows_refs, here_refs, refs = refs[:2], refs[2:4], refs[4:]
    near_refs, direct_refs, placer_ref = refs[: 2 * (low - 1)], refs[2 * (low - 1) : -1], refs[-1]
    batches, rows = ids_ref.shape
    width = rows_refs[0].shape[1]
    bucket = batches * capacity
    piece = high * bucket
    slots = experts * bucket
    earlier = (
        lax.broadcasted_iota(jnp.int32, (rows, rows), 0)
        < lax.broadcasted_iota(jnp.int32, (rows, rows), 1)
    )
    earlier = jnp.where(earlier, 1.0, 0.0).astype(jnp.bfloat16)
    for batch_index in range(batches):
        label = ids_ref[batch_index : batch_index + 1, :]
        named = lax.broadcasted_iota(jnp.int32, (experts, rows), 0) == label
        onehot = jnp.where(named, 1.0, 0.0)
        before = jnp.dot(onehot.astype(jnp.bfloat16), earlier, preferred_element_type=jnp.float32)
        rank = jnp.sum(before * onehot, axis=0, keepdims=True).astype(jnp.int32)
        away = label ^ me_ref[0]
        place = (away & (low - 1)) * high + (away >> (low.bit_length() - 1))
        slot = place * bucket + batch_index * capacity + rank
        hit = lax.broadcasted_iota(jnp.int32, (slots, rows), 0) == slot
        placer_ref[:, batch_index * rows : (batch_index + 1) * rows] = jnp.where(
            hit, 1.0, 0.0
        ).astype(jnp.bfloat16)
    for kind in range(2):
        placed = jnp.dot(
            placer_ref[...], rows_refs[kind][...], preferred_element_type=jnp.float32
        ).astype(jnp.bfloat16)
        here_refs[kind][...] = placed[:piece]
        for direct_ref, step in zip(direct_refs, direct_steps):
            direct_ref[:, kind * width : (kind + 1) * width] = placed[
                step * bucket : (step + 1) * bucket
            ]
        for step in range(1, low):
            near_refs[kind * (low - 1) + step - 1][...] = placed[
                step * piece : (step + 1) * piece
            ]


def body(cell_rows, cotangent, cluster_ids, enc_weight, up_weight, down_weight):
    experts = lax.axis_size("expert")
    dp_count = lax.axis_size("dp")
    me = lax.axis_index("expert")
    batch_count, local_rows, model_width = cell_rows.shape
    capacity = max(2, local_rows // 16)
    bucket = batch_count * capacity
    slot_count = experts * bucket
    all_rows = batch_count * local_rows
    high = min(4, experts)
    low = experts // high
    w_up = up_weight[0]
    w_down = down_weight[0]
    fence = lax.optimization_barrier

    vmem = pl.BlockSpec(memory_space=pltpu.VMEM)
    direct_steps = sorted({1, high - 1}, reverse=True)
    shapes = [(high * bucket, model_width)] * (2 * low)
    shapes += [(bucket, 2 * model_width)] * len(direct_steps)
    placed = pl.pallas_call(
        functools.partial(place_kernel, experts, low, high, capacity, direct_steps),
        out_shape=[jax.ShapeDtypeStruct(shape, jnp.bfloat16) for shape in shapes],
        in_specs=[pl.BlockSpec(memory_space=pltpu.SMEM), vmem, vmem, vmem],
        out_specs=[vmem] * len(shapes),
        scratch_shapes=[pltpu.VMEM((slot_count, all_rows), jnp.bfloat16)],
    )(
        me.astype(jnp.int32)[None],
        cluster_ids[:, :, 0],
        cell_rows.reshape(all_rows, model_width),
        cotangent.reshape(all_rows, model_width),
    )
    here, placed = placed[:2], placed[2:]
    cells_placed, grads_placed = placed[: low - 1], placed[low - 1 : 2 * (low - 1)]
    direct_placed = placed[2 * (low - 1) :]

    def copies(rows):
        pieces = []
        for shift in range(1, dp_count):
            ring = [(i, (i + shift) % dp_count) for i in range(dp_count)]
            pieces.append(lax.ppermute(rows, "dp", ring))
        return pieces

    def forward(features):
        pre_enc = jnp.dot(features, enc_weight, preferred_element_type=jnp.float32)
        silu_enc, slope_enc = silu_pair(pre_enc)
        encoded = features.astype(jnp.float32) + silu_enc
        inverse = lax.rsqrt(jnp.mean(encoded * encoded, axis=1, keepdims=True) + epsilon)
        norm_rows = (encoded * inverse).astype(jnp.bfloat16)
        pre_exp = jnp.dot(norm_rows, w_up, preferred_element_type=jnp.float32)
        silu_exp, slope_exp = silu_pair(pre_exp)
        return encoded, inverse, slope_enc, norm_rows, silu_exp.astype(jnp.bfloat16), slope_exp

    def stack(*pieces):
        return jnp.concatenate(pieces, axis=0)

    def send_near(pieces):
        return [swap(pieces[step - 1], step) for step in range(low - 1, 0, -1)]

    def far_pieces(own, near):
        return [
            stack(
                *[
                    piece[step * bucket : (step + 1) * bucket]
                    for piece in (near if step in direct_steps else [own] + near)
                ]
            )
            for step in range(high - 1, 0, -1)
        ]

    def send_far(pieces):
        return [swap(piece, step * low) for piece, step in zip(pieces, range(high - 1, 0, -1))]

    def here_and_near(own, near):
        return stack(*[piece[:bucket] for piece in [own] + near])

    cells_near = send_near(cells_placed)
    direct_placed, cells_near[-1] = fence((direct_placed, cells_near[-1]))
    direct = [swap(piece, step * low) for piece, step in zip(direct_placed, direct_steps)]
    cells_near, direct, here, grads_placed = fence((cells_near, direct, here, grads_placed))
    cells_first, direct, cells_far, grads_placed = fence(
        (
            here_and_near(here[0], cells_near),
            stack(*direct),
            far_pieces(here[0], cells_near),
            grads_placed,
        )
    )
    cells_first_copies = copies(cells_first)
    grads_near = send_near(grads_placed)
    cells_far = send_far(cells_far)
    direct_copies = copies(direct)
    grads_near, cells_first_copies = fence((grads_near, cells_first_copies))
    grads_first = here_and_near(here[1], grads_near)
    grads_first_copies = copies(grads_first)
    grads_far = send_far(far_pieces(here[1], grads_near))
    came = (cells_first_copies, direct_copies, grads_first_copies)
    cells_far, came = fence((cells_far, came))
    cells_far, came = fence((stack(*cells_far), came))
    cells_far_copies = copies(cells_far)
    features = stack(cells_first, direct[:, :model_width], cells_far)
    early = [
        (stack(cells, both[:, :model_width]), stack(grads, both[:, model_width:]))
        for cells, both, grads in zip(*came)
    ]
    grads_far, early, own_forward = fence((grads_far, early, forward(features)))
    grads_far, early, own_forward = fence((stack(*grads_far), early, own_forward))
    grads_far_copies = copies(grads_far)

    share = model_width // dp_count
    start = lax.axis_index("dp") * share
    block = share // experts

    def my_columns(rows):
        return lax.dynamic_slice_in_dim(rows, start, share, axis=1)

    stages = low.bit_length() - 1
    column = jnp.arange(share, dtype=jnp.int32)
    rank = column // block
    away = rank & (high - 1)
    away = away << stages
    for stage in range(stages):
        away = away | (((rank // high) >> (stages - 1 - stage)) & 1) << stage
    wanted = start + (away ^ me) * block + column % block
    picker = (jnp.arange(model_width, dtype=jnp.int32)[:, None] == wanted[None, :]).astype(
        jnp.bfloat16
    )

    norm_parts, pre_grad_parts, active_parts, grad_parts = [], [], [], []
    enc_parts = []

    def backward(features, grad_rows, values):
        encoded, inverse, slope_enc, norm_rows, active, slope_exp = values
        act_grad = jnp.dot(grad_rows, w_down, preferred_element_type=jnp.float32)
        pre_grad = (act_grad * slope_exp).astype(jnp.bfloat16)
        norm_grad = lax.dot_general(
            pre_grad, w_up, contract_last, preferred_element_type=jnp.float32
        )
        enc_rows_grad = inverse * norm_grad - inverse * inverse * inverse * encoded * jnp.mean(
            norm_grad * encoded, axis=1, keepdims=True
        )
        enc_pre_grad = (enc_rows_grad * slope_enc).astype(jnp.bfloat16)
        picked = jnp.dot(features, picker, preferred_element_type=jnp.float32).astype(jnp.bfloat16)
        enc_parts.append((picked, enc_pre_grad))
        norm_parts.append(my_columns(norm_rows))
        pre_grad_parts.append(pre_grad)
        active_parts.append(active)
        grad_parts.append(my_columns(grad_rows))

    backward(features, stack(grads_first, direct[:, model_width:], grads_far), own_forward)
    cells_far_copies, enc_parts[0] = fence((cells_far_copies, enc_parts[0]))
    for (cells_early, grads_early), cells_far, grads_far in zip(
        early, cells_far_copies, grads_far_copies
    ):
        features = stack(cells_early, cells_far)
        backward(features, stack(grads_early, grads_far), forward(features))

    def enc_terms(first, last):
        total = None
        for picked, enc_pre_grad in enc_parts:
            term = lax.dot_general(
                picked[:, first:last],
                enc_pre_grad,
                contract_rows,
                preferred_element_type=jnp.float32,
            )
            total = term if total is None else total + term
        return total

    kept = share
    total = None
    for stage in range(stages):
        kept //= 2
        if total is None:
            sent, total = enc_terms(kept, 2 * kept), enc_terms(0, kept)
        else:
            sent, total = total[kept:], total[:kept]
        total = total + swap(sent.astype(jnp.bfloat16), 1 << stage).astype(jnp.float32)
    if total is None:
        total = enc_terms(0, share)
    sent = total.astype(jnp.bfloat16)
    total = total[:block]
    for step in range(1, high):
        piece = sent[step * block : (step + 1) * block]
        total = total + swap(piece, step * low).astype(jnp.float32)

    def rows_product(left, right):
        return lax.dot_general(
            jnp.concatenate(left, axis=0),
            jnp.concatenate(right, axis=0),
            contract_rows,
            preferred_element_type=jnp.float32,
        ).astype(jnp.bfloat16)

    up_sum = rows_product(norm_parts, pre_grad_parts)
    down_sum = rows_product(grad_parts, active_parts)
    return (total, up_sum[None], down_sum[None])


def solution(mesh):
    in_specs = (
        P(None, ("dp", "expert"), None),
        P(None, ("dp", "expert"), None),
        P(None, ("dp", "expert"), None),
        P(),
        P("expert", None, None),
        P("expert", None, None),
    )
    out_specs = (P(("dp", "expert"), None), P("expert", "dp", None), P("expert", "dp", None))
    return jax.shard_map(body, mesh=mesh, in_specs=in_specs, out_specs=out_specs, check_vma=False)
```

```python
import functools

import jax
import jax.numpy as jnp
from jax import lax
from jax.experimental import pallas as pl
from jax.experimental.pallas import tpu as pltpu
from jax.sharding import PartitionSpec as P

epsilon = 1e-06
contract_rows = (((0,), (0,)), ((), ()))
contract_last = (((1,), (1,)), ((), ()))


def silu_pair(pre_value):
    gate_value = jax.nn.sigmoid(pre_value)
    return (pre_value * gate_value, gate_value * (1.0 + pre_value * (1.0 - gate_value)))


def swap(piece, distance):
    pairs = [(i, i ^ distance) for i in range(lax.axis_size("expert"))]
    return lax.ppermute(piece, "expert", pairs)


def place_kernel(experts, low, high, capacity, direct_steps, me_ref, ids_ref, *refs):
    rows_refs, here_refs, refs = refs[:2], refs[2:4], refs[4:]
    near_refs, direct_refs, placer_ref = refs[: 2 * (low - 1)], refs[2 * (low - 1) : -1], refs[-1]
    batches, rows = ids_ref.shape
    width = rows_refs[0].shape[1]
    bucket = batches * capacity
    piece = high * bucket
    slots = experts * bucket
    earlier = (
        lax.broadcasted_iota(jnp.int32, (rows, rows), 0)
        < lax.broadcasted_iota(jnp.int32, (rows, rows), 1)
    )
    earlier = jnp.where(earlier, 1.0, 0.0).astype(jnp.bfloat16)
    for batch_index in range(batches):
        label = ids_ref[batch_index : batch_index + 1, :]
        named = lax.broadcasted_iota(jnp.int32, (experts, rows), 0) == label
        onehot = jnp.where(named, 1.0, 0.0)
        before = jnp.dot(onehot.astype(jnp.bfloat16), earlier, preferred_element_type=jnp.float32)
        rank = jnp.sum(before * onehot, axis=0, keepdims=True).astype(jnp.int32)
        away = label ^ me_ref[0]
        place = (away & (low - 1)) * high + (away >> (low.bit_length() - 1))
        slot = place * bucket + batch_index * capacity + rank
        hit = lax.broadcasted_iota(jnp.int32, (slots, rows), 0) == slot
        placer_ref[:, batch_index * rows : (batch_index + 1) * rows] = jnp.where(
            hit, 1.0, 0.0
        ).astype(jnp.bfloat16)
    for kind in range(2):
        placed = jnp.dot(
            placer_ref[...], rows_refs[kind][...], preferred_element_type=jnp.float32
        ).astype(jnp.bfloat16)
        here_refs[kind][...] = placed[:piece]
        for direct_ref, step in zip(direct_refs, direct_steps):
            direct_ref[:, kind * width : (kind + 1) * width] = placed[
                step * bucket : (step + 1) * bucket
            ]
        for step in range(1, low):
            near_refs[kind * (low - 1) + step - 1][...] = placed[
                step * piece : (step + 1) * piece
            ]


def body(cell_rows, cotangent, cluster_ids, enc_weight, up_weight, down_weight):
    experts = lax.axis_size("expert")
    dp_count = lax.axis_size("dp")
    me = lax.axis_index("expert")
    batch_count, local_rows, model_width = cell_rows.shape
    capacity = max(2, local_rows // 16)
    bucket = batch_count * capacity
    slot_count = experts * bucket
    all_rows = batch_count * local_rows
    high = min(4, experts)
    low = experts // high
    w_up = up_weight[0]
    w_down = down_weight[0]
    fence = lax.optimization_barrier

    vmem = pl.BlockSpec(memory_space=pltpu.VMEM)
    direct_steps = sorted({1, high - 1}, reverse=True)
    shapes = [(high * bucket, model_width)] * (2 * low)
    shapes += [(bucket, 2 * model_width)] * len(direct_steps)
    placed = pl.pallas_call(
        functools.partial(place_kernel, experts, low, high, capacity, direct_steps),
        out_shape=[jax.ShapeDtypeStruct(shape, jnp.bfloat16) for shape in shapes],
        in_specs=[pl.BlockSpec(memory_space=pltpu.SMEM), vmem, vmem, vmem],
        out_specs=[vmem] * len(shapes),
        scratch_shapes=[pltpu.VMEM((slot_count, all_rows), jnp.bfloat16)],
    )(
        me.astype(jnp.int32)[None],
        cluster_ids[:, :, 0],
        cell_rows.reshape(all_rows, model_width),
        cotangent.reshape(all_rows, model_width),
    )
    here, placed = placed[:2], placed[2:]
    cells_placed, grads_placed = placed[: low - 1], placed[low - 1 : 2 * (low - 1)]
    direct_placed = placed[2 * (low - 1) :]

    def copies(rows):
        pieces = []
        for shift in range(1, dp_count):
            ring = [(i, (i + shift) % dp_count) for i in range(dp_count)]
            pieces.append(lax.ppermute(rows, "dp", ring))
        return pieces

    def forward(features):
        pre_enc = jnp.dot(features, enc_weight, preferred_element_type=jnp.float32)
        silu_enc, slope_enc = silu_pair(pre_enc)
        encoded = features.astype(jnp.float32) + silu_enc
        inverse = lax.rsqrt(jnp.mean(encoded * encoded, axis=1, keepdims=True) + epsilon)
        norm_rows = (encoded * inverse).astype(jnp.bfloat16)
        pre_exp = jnp.dot(norm_rows, w_up, preferred_element_type=jnp.float32)
        silu_exp, slope_exp = silu_pair(pre_exp)
        return encoded, inverse, slope_enc, norm_rows, silu_exp.astype(jnp.bfloat16), slope_exp

    def stack(*pieces):
        return jnp.concatenate(pieces, axis=0)

    def send_near(pieces):
        return [swap(pieces[step - 1], step) for step in range(low - 1, 0, -1)]

    def far_pieces(own, near):
        return [
            stack(
                *[
                    piece[step * bucket : (step + 1) * bucket]
                    for piece in (near if step in direct_steps else [own] + near)
                ]
            )
            for step in range(high - 1, 0, -1)
        ]

    def send_far(pieces):
        return [swap(piece, step * low) for piece, step in zip(pieces, range(high - 1, 0, -1))]

    def here_and_near(own, near):
        return stack(*[piece[:bucket] for piece in [own] + near])

    cells_near = send_near(cells_placed)
    direct_placed, cells_near[-1] = fence((direct_placed, cells_near[-1]))
    direct = [swap(piece, step * low) for piece, step in zip(direct_placed, direct_steps)]
    cells_near, direct, here, grads_placed = fence((cells_near, direct, here, grads_placed))
    cells_first, direct, cells_far, grads_placed = fence(
        (
            here_and_near(here[0], cells_near),
            stack(*direct),
            far_pieces(here[0], cells_near),
            grads_placed,
        )
    )
    cells_first_copies = copies(cells_first)
    grads_near = send_near(grads_placed)
    cells_far = send_far(cells_far)
    direct_cells, direct_grads = direct[:, :model_width], direct[:, model_width:]
    grads_near, cells_first_copies = fence((grads_near, cells_first_copies))
    grads_first = here_and_near(here[1], grads_near)
    grads_far = far_pieces(here[1], grads_near)
    second_copies = copies(stack(grads_first, direct_cells, direct_grads))
    *grads_far, grads_last = send_far(grads_far[:-1]) + grads_far[-1:]
    came = (cells_first_copies, second_copies)
    cells_far, came, grads_last = fence((cells_far, came, grads_last))
    cells_far, came, grads_last = fence((stack(*cells_far), came, grads_last))
    cells_far_copies = copies(cells_far)
    grads_far += [swap(grads_last, low)]
    features = stack(cells_first, direct_cells, cells_far)
    first_rows, direct_rows = cells_first.shape[0], direct.shape[0]
    early = [
        (
            stack(cells, second[first_rows:-direct_rows]),
            stack(second[:first_rows], second[-direct_rows:]),
        )
        for cells, second in zip(*came)
    ]
    grads_far, early, own_forward = fence((grads_far, early, forward(features)))
    grads_far, early, own_forward = fence((stack(*grads_far), early, own_forward))
    grads_far_copies = copies(grads_far)

    share = model_width // dp_count
    start = lax.axis_index("dp") * share
    block = share // experts

    def my_columns(rows):
        return lax.dynamic_slice_in_dim(rows, start, share, axis=1)

    stages = low.bit_length() - 1
    column = jnp.arange(share, dtype=jnp.int32)
    rank = column // block
    away = rank & (high - 1)
    away = away << stages
    for stage in range(stages):
        away = away | (((rank // high) >> (stages - 1 - stage)) & 1) << stage
    wanted = start + (away ^ me) * block + column % block
    picker = (jnp.arange(model_width, dtype=jnp.int32)[:, None] == wanted[None, :]).astype(
        jnp.bfloat16
    )

    norm_parts, pre_grad_parts, active_parts, grad_parts = [], [], [], []
    enc_parts = []

    def backward(features, grad_rows, values):
        encoded, inverse, slope_enc, norm_rows, active, slope_exp = values
        act_grad = jnp.dot(grad_rows, w_down, preferred_element_type=jnp.float32)
        pre_grad = (act_grad * slope_exp).astype(jnp.bfloat16)
        norm_grad = lax.dot_general(
            pre_grad, w_up, contract_last, preferred_element_type=jnp.float32
        )
        enc_rows_grad = inverse * norm_grad - inverse * inverse * inverse * encoded * jnp.mean(
            norm_grad * encoded, axis=1, keepdims=True
        )
        enc_pre_grad = (enc_rows_grad * slope_enc).astype(jnp.bfloat16)
        picked = jnp.dot(features, picker, preferred_element_type=jnp.float32).astype(jnp.bfloat16)
        enc_parts.append((picked, enc_pre_grad))
        norm_parts.append(my_columns(norm_rows))
        pre_grad_parts.append(pre_grad)
        active_parts.append(active)
        grad_parts.append(my_columns(grad_rows))

    backward(features, stack(grads_first, direct_grads, grads_far), own_forward)
    cells_far_copies, enc_parts[0] = fence((cells_far_copies, enc_parts[0]))
    for (cells_early, grads_early), cells_far, grads_far in zip(
        early, cells_far_copies, grads_far_copies
    ):
        features = stack(cells_early, cells_far)
        backward(features, stack(grads_early, grads_far), forward(features))

    def enc_terms(first, last):
        total = None
        for picked, enc_pre_grad in enc_parts:
            term = lax.dot_general(
                picked[:, first:last],
                enc_pre_grad,
                contract_rows,
                preferred_element_type=jnp.float32,
            )
            total = term if total is None else total + term
        return total

    kept = share
    total = None
    for stage in range(stages):
        kept //= 2
        if total is None:
            sent, total = enc_terms(kept, 2 * kept), enc_terms(0, kept)
        else:
            sent, total = total[kept:], total[:kept]
        total = total + swap(sent.astype(jnp.bfloat16), 1 << stage).astype(jnp.float32)
    if total is None:
        total = enc_terms(0, share)
    sent = total.astype(jnp.bfloat16)
    total = total[:block]
    for step in range(1, high):
        piece = sent[step * block : (step + 1) * block]
        total = total + swap(piece, step * low).astype(jnp.float32)

    def rows_product(left, right):
        return lax.dot_general(
            jnp.concatenate(left, axis=0),
            jnp.concatenate(right, axis=0),
            contract_rows,
            preferred_element_type=jnp.float32,
        ).astype(jnp.bfloat16)

    up_sum = rows_product(norm_parts, pre_grad_parts)
    down_sum = rows_product(grad_parts, active_parts)
    return (total, up_sum[None], down_sum[None])


def solution(mesh):
    in_specs = (
        P(None, ("dp", "expert"), None),
        P(None, ("dp", "expert"), None),
        P(None, ("dp", "expert"), None),
        P(),
        P("expert", None, None),
        P("expert", None, None),
    )
    out_specs = (P(("dp", "expert"), None), P("expert", "dp", None), P("expert", "dp", None))
    return jax.shard_map(body, mesh=mesh, in_specs=in_specs, out_specs=out_specs, check_vma=False)
```

```python
import functools

import jax
import jax.numpy as jnp
from jax import lax
from jax.experimental import pallas as pl
from jax.experimental.pallas import tpu as pltpu
from jax.sharding import PartitionSpec as P

epsilon = 1e-06
contract_rows = (((0,), (0,)), ((), ()))
contract_last = (((1,), (1,)), ((), ()))


def silu_pair(pre_value):
    gate_value = jax.nn.sigmoid(pre_value)
    return (pre_value * gate_value, gate_value * (1.0 + pre_value * (1.0 - gate_value)))


def swap(piece, distance):
    pairs = [(i, i ^ distance) for i in range(lax.axis_size("expert"))]
    return lax.ppermute(piece, "expert", pairs)


def place_kernel(experts, low, high, capacity, direct_steps, me_ref, ids_ref, *refs):
    rows_refs, here_refs, refs = refs[:2], refs[2:4], refs[4:]
    near_refs, direct_refs, placer_ref = refs[: 2 * (low - 1)], refs[2 * (low - 1) : -1], refs[-1]
    batches, rows = ids_ref.shape
    width = rows_refs[0].shape[1]
    bucket = batches * capacity
    piece = high * bucket
    slots = experts * bucket
    earlier = (
        lax.broadcasted_iota(jnp.int32, (rows, rows), 0)
        < lax.broadcasted_iota(jnp.int32, (rows, rows), 1)
    )
    earlier = jnp.where(earlier, 1.0, 0.0).astype(jnp.bfloat16)
    for batch_index in range(batches):
        label = ids_ref[batch_index : batch_index + 1, :]
        named = lax.broadcasted_iota(jnp.int32, (experts, rows), 0) == label
        onehot = jnp.where(named, 1.0, 0.0)
        before = jnp.dot(onehot.astype(jnp.bfloat16), earlier, preferred_element_type=jnp.float32)
        rank = jnp.sum(before * onehot, axis=0, keepdims=True).astype(jnp.int32)
        away = label ^ me_ref[0]
        place = (away & (low - 1)) * high + (away >> (low.bit_length() - 1))
        slot = place * bucket + batch_index * capacity + rank
        hit = lax.broadcasted_iota(jnp.int32, (slots, rows), 0) == slot
        placer_ref[:, batch_index * rows : (batch_index + 1) * rows] = jnp.where(
            hit, 1.0, 0.0
        ).astype(jnp.bfloat16)
    for kind in range(2):
        placed = jnp.dot(
            placer_ref[...], rows_refs[kind][...], preferred_element_type=jnp.float32
        ).astype(jnp.bfloat16)
        here_refs[kind][...] = placed[:piece]
        for direct_ref, step in zip(direct_refs, direct_steps):
            direct_ref[:, kind * width : (kind + 1) * width] = placed[
                step * bucket : (step + 1) * bucket
            ]
        for step in range(1, low):
            near_refs[kind * (low - 1) + step - 1][...] = placed[
                step * piece : (step + 1) * piece
            ]


def body(cell_rows, cotangent, cluster_ids, enc_weight, up_weight, down_weight):
    experts = lax.axis_size("expert")
    dp_count = lax.axis_size("dp")
    me = lax.axis_index("expert")
    batch_count, local_rows, model_width = cell_rows.shape
    capacity = max(2, local_rows // 16)
    bucket = batch_count * capacity
    slot_count = experts * bucket
    all_rows = batch_count * local_rows
    high = min(4, experts)
    low = experts // high
    w_up = up_weight[0]
    w_down = down_weight[0]
    fence = lax.optimization_barrier

    vmem = pl.BlockSpec(memory_space=pltpu.VMEM)
    direct_steps = sorted({1, high - 1}, reverse=True)
    shapes = [(high * bucket, model_width)] * (2 * low)
    shapes += [(bucket, 2 * model_width)] * len(direct_steps)
    placed = pl.pallas_call(
        functools.partial(place_kernel, experts, low, high, capacity, direct_steps),
        out_shape=[jax.ShapeDtypeStruct(shape, jnp.bfloat16) for shape in shapes],
        in_specs=[pl.BlockSpec(memory_space=pltpu.SMEM), vmem, vmem, vmem],
        out_specs=[vmem] * len(shapes),
        scratch_shapes=[pltpu.VMEM((slot_count, all_rows), jnp.bfloat16)],
    )(
        me.astype(jnp.int32)[None],
        cluster_ids[:, :, 0],
        cell_rows.reshape(all_rows, model_width),
        cotangent.reshape(all_rows, model_width),
    )
    here, placed = placed[:2], placed[2:]
    cells_placed, grads_placed = placed[: low - 1], placed[low - 1 : 2 * (low - 1)]
    direct_placed = placed[2 * (low - 1) :]

    def copies(rows):
        pieces = []
        for shift in range(1, dp_count):
            ring = [(i, (i + shift) % dp_count) for i in range(dp_count)]
            pieces.append(lax.ppermute(rows, "dp", ring))
        return pieces

    def forward(features):
        pre_enc = jnp.dot(features, enc_weight, preferred_element_type=jnp.float32)
        silu_enc, slope_enc = silu_pair(pre_enc)
        encoded = features.astype(jnp.float32) + silu_enc
        inverse = lax.rsqrt(jnp.mean(encoded * encoded, axis=1, keepdims=True) + epsilon)
        norm_rows = (encoded * inverse).astype(jnp.bfloat16)
        pre_exp = jnp.dot(norm_rows, w_up, preferred_element_type=jnp.float32)
        silu_exp, slope_exp = silu_pair(pre_exp)
        return encoded, inverse, slope_enc, norm_rows, silu_exp.astype(jnp.bfloat16), slope_exp

    def stack(*pieces):
        return jnp.concatenate(pieces, axis=0)

    def send_near(pieces):
        return [swap(pieces[step - 1], step) for step in range(low - 1, 0, -1)]

    def far_pieces(own, near):
        return [
            stack(
                *[
                    piece[step * bucket : (step + 1) * bucket]
                    for piece in (near if step in direct_steps else [own] + near)
                ]
            )
            for step in range(high - 1, 0, -1)
        ]

    def send_far(pieces):
        return [swap(piece, step * low) for piece, step in zip(pieces, range(high - 1, 0, -1))]

    def here_and_near(own, near):
        return stack(*[piece[:bucket] for piece in [own] + near])

    cells_near = send_near(cells_placed)
    direct_placed, cells_near[-1] = fence((direct_placed, cells_near[-1]))
    direct = [swap(piece, step * low) for piece, step in zip(direct_placed, direct_steps)]
    cells_near, direct, here, grads_placed = fence((cells_near, direct, here, grads_placed))
    cells_first, direct, cells_far, grads_placed = fence(
        (
            here_and_near(here[0], cells_near),
            stack(*direct),
            far_pieces(here[0], cells_near),
            grads_placed,
        )
    )
    cells_first_copies = copies(cells_first)
    grads_near = send_near(grads_placed)
    cells_far = send_far(cells_far)
    direct_cells, direct_grads = direct[:, :model_width], direct[:, model_width:]
    grads_first = here_and_near(here[1], grads_near)
    second_copies = copies(stack(grads_first, direct_cells, direct_grads))
    grads_far = far_pieces(here[1], grads_near)
    cells_far[:-1], grads_far = fence((cells_far[:-1], grads_far))
    grads_far = send_far(grads_far)
    came = (cells_first_copies, second_copies)
    cells_far, came = fence((cells_far, came))
    cells_far, came = fence((stack(*cells_far), came))
    cells_far_copies = copies(cells_far)
    features = stack(cells_first, direct_cells, cells_far)
    first_rows, direct_rows = cells_first.shape[0], direct.shape[0]
    early = [
        (
            stack(cells, second[first_rows:-direct_rows]),
            stack(second[:first_rows], second[-direct_rows:]),
        )
        for cells, second in zip(*came)
    ]
    grads_far, early, own_forward = fence((grads_far, early, forward(features)))
    grads_far, early, own_forward = fence((stack(*grads_far), early, own_forward))
    grads_far_copies = copies(grads_far)

    share = model_width // dp_count
    start = lax.axis_index("dp") * share
    block = share // experts

    def my_columns(rows):
        return lax.dynamic_slice_in_dim(rows, start, share, axis=1)

    stages = low.bit_length() - 1
    column = jnp.arange(share, dtype=jnp.int32)
    rank = column // block
    away = rank & (high - 1)
    away = away << stages
    for stage in range(stages):
        away = away | (((rank // high) >> (stages - 1 - stage)) & 1) << stage
    wanted = start + (away ^ me) * block + column % block
    picker = (jnp.arange(model_width, dtype=jnp.int32)[:, None] == wanted[None, :]).astype(
        jnp.bfloat16
    )

    norm_parts, pre_grad_parts, active_parts, grad_parts = [], [], [], []
    enc_parts = []

    def backward(features, grad_rows, values):
        encoded, inverse, slope_enc, norm_rows, active, slope_exp = values
        act_grad = jnp.dot(grad_rows, w_down, preferred_element_type=jnp.float32)
        pre_grad = (act_grad * slope_exp).astype(jnp.bfloat16)
        norm_grad = lax.dot_general(
            pre_grad, w_up, contract_last, preferred_element_type=jnp.float32
        )
        enc_rows_grad = inverse * norm_grad - inverse * inverse * inverse * encoded * jnp.mean(
            norm_grad * encoded, axis=1, keepdims=True
        )
        enc_pre_grad = (enc_rows_grad * slope_enc).astype(jnp.bfloat16)
        picked = jnp.dot(features, picker, preferred_element_type=jnp.float32).astype(jnp.bfloat16)
        enc_parts.append((picked, enc_pre_grad))
        norm_parts.append(my_columns(norm_rows))
        pre_grad_parts.append(pre_grad)
        active_parts.append(active)
        grad_parts.append(my_columns(grad_rows))

    backward(features, stack(grads_first, direct_grads, grads_far), own_forward)
    cells_far_copies, enc_parts[0] = fence((cells_far_copies, enc_parts[0]))
    for (cells_early, grads_early), cells_far, grads_far in zip(
        early, cells_far_copies, grads_far_copies
    ):
        features = stack(cells_early, cells_far)
        backward(features, stack(grads_early, grads_far), forward(features))

    def enc_terms(first, last):
        total = None
        for picked, enc_pre_grad in enc_parts:
            term = lax.dot_general(
                picked[:, first:last],
                enc_pre_grad,
                contract_rows,
                preferred_element_type=jnp.float32,
            )
            total = term if total is None else total + term
        return total

    kept = share
    total = None
    for stage in range(stages):
        kept //= 2
        if total is None:
            sent, total = enc_terms(kept, 2 * kept), enc_terms(0, kept)
        else:
            sent, total = total[kept:], total[:kept]
        total = total + swap(sent.astype(jnp.bfloat16), 1 << stage).astype(jnp.float32)
    if total is None:
        total = enc_terms(0, share)
    sent = total.astype(jnp.bfloat16)
    total = total[:block]
    for step in range(1, high):
        piece = sent[step * block : (step + 1) * block]
        total = total + swap(piece, step * low).astype(jnp.float32)

    def rows_product(left, right):
        return lax.dot_general(
            jnp.concatenate(left, axis=0),
            jnp.concatenate(right, axis=0),
            contract_rows,
            preferred_element_type=jnp.float32,
        ).astype(jnp.bfloat16)

    up_sum = rows_product(norm_parts, pre_grad_parts)
    down_sum = rows_product(grad_parts, active_parts)
    return (total, up_sum[None], down_sum[None])


def solution(mesh):
    in_specs = (
        P(None, ("dp", "expert"), None),
        P(None, ("dp", "expert"), None),
        P(None, ("dp", "expert"), None),
        P(),
        P("expert", None, None),
        P("expert", None, None),
    )
    out_specs = (P(("dp", "expert"), None), P("expert", "dp", None), P("expert", "dp", None))
    return jax.shard_map(body, mesh=mesh, in_specs=in_specs, out_specs=out_specs, check_vma=False)
```

```python
import functools

import jax
import jax.numpy as jnp
from jax import lax
from jax.experimental import pallas as pl
from jax.experimental.pallas import tpu as pltpu
from jax.sharding import PartitionSpec as P

epsilon = 1e-06
contract_rows = (((0,), (0,)), ((), ()))
contract_last = (((1,), (1,)), ((), ()))


def silu_pair(pre_value):
    gate_value = jax.nn.sigmoid(pre_value)
    return (pre_value * gate_value, gate_value * (1.0 + pre_value * (1.0 - gate_value)))


def swap(piece, distance):
    pairs = [(i, i ^ distance) for i in range(lax.axis_size("expert"))]
    return lax.ppermute(piece, "expert", pairs)


def place_kernel(experts, low, high, capacity, direct_steps, me_ref, ids_ref, *refs):
    rows_refs, here_refs, refs = refs[:2], refs[2:4], refs[4:]
    near_refs, direct_refs, placer_ref = refs[: 2 * (low - 1)], refs[2 * (low - 1) : -1], refs[-1]
    batches, rows = ids_ref.shape
    width = rows_refs[0].shape[1]
    bucket = batches * capacity
    piece = high * bucket
    slots = experts * bucket
    earlier = (
        lax.broadcasted_iota(jnp.int32, (rows, rows), 0)
        < lax.broadcasted_iota(jnp.int32, (rows, rows), 1)
    )
    earlier = jnp.where(earlier, 1.0, 0.0).astype(jnp.bfloat16)
    for batch_index in range(batches):
        label = ids_ref[batch_index : batch_index + 1, :]
        named = lax.broadcasted_iota(jnp.int32, (experts, rows), 0) == label
        onehot = jnp.where(named, 1.0, 0.0)
        before = jnp.dot(onehot.astype(jnp.bfloat16), earlier, preferred_element_type=jnp.float32)
        rank = jnp.sum(before * onehot, axis=0, keepdims=True).astype(jnp.int32)
        away = label ^ me_ref[0]
        place = (away & (low - 1)) * high + (away >> (low.bit_length() - 1))
        slot = place * bucket + batch_index * capacity + rank
        hit = lax.broadcasted_iota(jnp.int32, (slots, rows), 0) == slot
        placer_ref[:, batch_index * rows : (batch_index + 1) * rows] = jnp.where(
            hit, 1.0, 0.0
        ).astype(jnp.bfloat16)
    for kind in range(2):
        placed = jnp.dot(
            placer_ref[...], rows_refs[kind][...], preferred_element_type=jnp.float32
        ).astype(jnp.bfloat16)
        here_refs[kind][...] = placed[:piece]
        for direct_ref, step in zip(direct_refs, direct_steps):
            direct_ref[:, kind * width : (kind + 1) * width] = placed[
                step * bucket : (step + 1) * bucket
            ]
        for step in range(1, low):
            near_refs[kind * (low - 1) + step - 1][...] = placed[
                step * piece : (step + 1) * piece
            ]


def body(cell_rows, cotangent, cluster_ids, enc_weight, up_weight, down_weight):
    experts = lax.axis_size("expert")
    dp_count = lax.axis_size("dp")
    me = lax.axis_index("expert")
    batch_count, local_rows, model_width = cell_rows.shape
    capacity = max(2, local_rows // 16)
    bucket = batch_count * capacity
    slot_count = experts * bucket
    all_rows = batch_count * local_rows
    high = min(4, experts)
    low = experts // high
    w_up = up_weight[0]
    w_down = down_weight[0]
    fence = lax.optimization_barrier

    vmem = pl.BlockSpec(memory_space=pltpu.VMEM)
    direct_steps = sorted({1, high - 1}, reverse=True)
    shapes = [(high * bucket, model_width)] * (2 * low)
    shapes += [(bucket, 2 * model_width)] * len(direct_steps)
    placed = pl.pallas_call(
        functools.partial(place_kernel, experts, low, high, capacity, direct_steps),
        out_shape=[jax.ShapeDtypeStruct(shape, jnp.bfloat16) for shape in shapes],
        in_specs=[pl.BlockSpec(memory_space=pltpu.SMEM), vmem, vmem, vmem],
        out_specs=[vmem] * len(shapes),
        scratch_shapes=[pltpu.VMEM((slot_count, all_rows), jnp.bfloat16)],
    )(
        me.astype(jnp.int32)[None],
        cluster_ids[:, :, 0],
        cell_rows.reshape(all_rows, model_width),
        cotangent.reshape(all_rows, model_width),
    )
    here, placed = placed[:2], placed[2:]
    cells_placed, grads_placed = placed[: low - 1], list(placed[low - 1 : 2 * (low - 1)])
    direct_placed = placed[2 * (low - 1) :]

    def copies(rows):
        pieces = []
        for shift in range(1, dp_count):
            ring = [(i, (i + shift) % dp_count) for i in range(dp_count)]
            pieces.append(lax.ppermute(rows, "dp", ring))
        return pieces

    def forward(features):
        pre_enc = jnp.dot(features, enc_weight, preferred_element_type=jnp.float32)
        silu_enc, slope_enc = silu_pair(pre_enc)
        encoded = features.astype(jnp.float32) + silu_enc
        inverse = lax.rsqrt(jnp.mean(encoded * encoded, axis=1, keepdims=True) + epsilon)
        norm_rows = (encoded * inverse).astype(jnp.bfloat16)
        pre_exp = jnp.dot(norm_rows, w_up, preferred_element_type=jnp.float32)
        silu_exp, slope_exp = silu_pair(pre_exp)
        return encoded, inverse, slope_enc, norm_rows, silu_exp.astype(jnp.bfloat16), slope_exp

    def stack(*pieces):
        return jnp.concatenate(pieces, axis=0)

    def send_near(pieces, first=1):
        return [swap(pieces[step - first], step) for step in range(low - 1, first - 1, -1)]

    def far_pieces(own, near):
        return [
            stack(
                *[
                    piece[step * bucket : (step + 1) * bucket]
                    for piece in (near if step in direct_steps else [own] + near)
                ]
            )
            for step in range(high - 1, 0, -1)
        ]

    def send_far(pieces):
        return [swap(piece, step * low) for piece, step in zip(pieces, range(high - 1, 0, -1))]

    def here_and_near(own, near):
        return stack(*[piece[:bucket] for piece in [own] + near])

    cells_near = send_near(cells_placed)
    direct_placed, grads_placed[0], cells_near[-1] = fence(
        (direct_placed, grads_placed[0], cells_near[-1])
    )
    grads_near_last = swap(grads_placed[0], 1)
    direct = [swap(piece, step * low) for piece, step in zip(direct_placed, direct_steps)]
    cells_near, direct, here, grads_placed, grads_near_last = fence(
        (cells_near, direct, here, grads_placed[1:], grads_near_last)
    )
    cells_first, direct, cells_far, grads_placed, grads_near_last = fence(
        (
            here_and_near(here[0], cells_near),
            stack(*direct),
            far_pieces(here[0], cells_near),
            grads_placed,
            grads_near_last,
        )
    )
    cells_first_copies = copies(cells_first)
    grads_near = send_near(grads_placed, 2) + [grads_near_last]
    cells_far[-1], cells_first_copies = fence((cells_far[-1], cells_first_copies))
    cells_far = send_far(cells_far)
    direct_cells, direct_grads = direct[:, :model_width], direct[:, model_width:]
    grads_first = here_and_near(here[1], grads_near)
    second_copies = copies(stack(grads_first, direct_cells, direct_grads))
    grads_far = far_pieces(here[1], grads_near)
    cells_far[:-1], grads_far = fence((cells_far[:-1], grads_far))
    grads_far = send_far(grads_far)
    came = (cells_first_copies, second_copies)
    cells_far, came = fence((cells_far, came))
    cells_far, came = fence((stack(*cells_far), came))
    cells_far_copies = copies(cells_far)
    features = stack(cells_first, direct_cells, cells_far)
    first_rows, direct_rows = cells_first.shape[0], direct.shape[0]
    early = [
        (
            stack(cells, second[first_rows:-direct_rows]),
            stack(second[:first_rows], second[-direct_rows:]),
        )
        for cells, second in zip(*came)
    ]
    grads_far, early, own_forward = fence((grads_far, early, forward(features)))
    grads_far, early, own_forward = fence((stack(*grads_far), early, own_forward))
    grads_far_copies = copies(grads_far)

    share = model_width // dp_count
    start = lax.axis_index("dp") * share
    block = share // experts

    def my_columns(rows):
        return lax.dynamic_slice_in_dim(rows, start, share, axis=1)

    stages = low.bit_length() - 1
    column = jnp.arange(share, dtype=jnp.int32)
    rank = column // block
    away = rank & (high - 1)
    away = away << stages
    for stage in range(stages):
        away = away | (((rank // high) >> (stages - 1 - stage)) & 1) << stage
    wanted = start + (away ^ me) * block + column % block
    picker = (jnp.arange(model_width, dtype=jnp.int32)[:, None] == wanted[None, :]).astype(
        jnp.bfloat16
    )

    norm_parts, pre_grad_parts, active_parts, grad_parts = [], [], [], []
    enc_parts = []

    def backward(features, grad_rows, values):
        encoded, inverse, slope_enc, norm_rows, active, slope_exp = values
        act_grad = jnp.dot(grad_rows, w_down, preferred_element_type=jnp.float32)
        pre_grad = (act_grad * slope_exp).astype(jnp.bfloat16)
        norm_grad = lax.dot_general(
            pre_grad, w_up, contract_last, preferred_element_type=jnp.float32
        )
        enc_rows_grad = inverse * norm_grad - inverse * inverse * inverse * encoded * jnp.mean(
            norm_grad * encoded, axis=1, keepdims=True
        )
        enc_pre_grad = (enc_rows_grad * slope_enc).astype(jnp.bfloat16)
        picked = jnp.dot(features, picker, preferred_element_type=jnp.float32).astype(jnp.bfloat16)
        enc_parts.append((picked, enc_pre_grad))
        norm_parts.append(my_columns(norm_rows))
        pre_grad_parts.append(pre_grad)
        active_parts.append(active)
        grad_parts.append(my_columns(grad_rows))

    backward(features, stack(grads_first, direct_grads, grads_far), own_forward)
    cells_far_copies, enc_parts[0] = fence((cells_far_copies, enc_parts[0]))
    for (cells_early, grads_early), cells_far, grads_far in zip(
        early, cells_far_copies, grads_far_copies
    ):
        features = stack(cells_early, cells_far)
        backward(features, stack(grads_early, grads_far), forward(features))

    def enc_terms(first, last):
        total = None
        for picked, enc_pre_grad in enc_parts:
            term = lax.dot_general(
                picked[:, first:last],
                enc_pre_grad,
                contract_rows,
                preferred_element_type=jnp.float32,
            )
            total = term if total is None else total + term
        return total

    kept = share
    total = None
    for stage in range(stages):
        kept //= 2
        if total is None:
            sent, total = enc_terms(kept, 2 * kept), enc_terms(0, kept)
        else:
            sent, total = total[kept:], total[:kept]
        total = total + swap(sent.astype(jnp.bfloat16), 1 << stage).astype(jnp.float32)
    if total is None:
        total = enc_terms(0, share)
    sent = total.astype(jnp.bfloat16)
    total = total[:block]
    for step in range(1, high):
        piece = sent[step * block : (step + 1) * block]
        total = total + swap(piece, step * low).astype(jnp.float32)

    def rows_product(left, right):
        return lax.dot_general(
            jnp.concatenate(left, axis=0),
            jnp.concatenate(right, axis=0),
            contract_rows,
            preferred_element_type=jnp.float32,
        ).astype(jnp.bfloat16)

    up_sum = rows_product(norm_parts, pre_grad_parts)
    down_sum = rows_product(grad_parts, active_parts)
    return (total, up_sum[None], down_sum[None])


def solution(mesh):
    in_specs = (
        P(None, ("dp", "expert"), None),
        P(None, ("dp", "expert"), None),
        P(None, ("dp", "expert"), None),
        P(),
        P("expert", None, None),
        P("expert", None, None),
    )
    out_specs = (P(("dp", "expert"), None), P("expert", "dp", None), P("expert", "dp", None))
    return jax.shard_map(body, mesh=mesh, in_specs=in_specs, out_specs=out_specs, check_vma=False)
```

```python
import functools

import jax
import jax.numpy as jnp
from jax import lax
from jax.experimental import pallas as pl
from jax.experimental.pallas import tpu as pltpu
from jax.sharding import PartitionSpec as P

epsilon = 1e-06
contract_rows = (((0,), (0,)), ((), ()))
contract_last = (((1,), (1,)), ((), ()))


def silu_pair(pre_value):
    gate_value = jax.nn.sigmoid(pre_value)
    return (pre_value * gate_value, gate_value * (1.0 + pre_value * (1.0 - gate_value)))


def swap(piece, distance):
    pairs = [(i, i ^ distance) for i in range(lax.axis_size("expert"))]
    return lax.ppermute(piece, "expert", pairs)


def place_kernel(experts, low, high, capacity, direct_steps, me_ref, ids_ref, *refs):
    rows_refs, here_refs, refs = refs[:2], refs[2:4], refs[4:]
    near_refs, direct_refs, placer_ref = refs[: 2 * (low - 1)], refs[2 * (low - 1) : -1], refs[-1]
    batches, rows = ids_ref.shape
    width = rows_refs[0].shape[1]
    bucket = batches * capacity
    piece = high * bucket
    slots = experts * bucket
    earlier = (
        lax.broadcasted_iota(jnp.int32, (rows, rows), 0)
        < lax.broadcasted_iota(jnp.int32, (rows, rows), 1)
    )
    earlier = jnp.where(earlier, 1.0, 0.0).astype(jnp.bfloat16)
    for batch_index in range(batches):
        label = ids_ref[batch_index : batch_index + 1, :]
        named = lax.broadcasted_iota(jnp.int32, (experts, rows), 0) == label
        onehot = jnp.where(named, 1.0, 0.0)
        before = jnp.dot(onehot.astype(jnp.bfloat16), earlier, preferred_element_type=jnp.float32)
        rank = jnp.sum(before * onehot, axis=0, keepdims=True).astype(jnp.int32)
        away = label ^ me_ref[0]
        place = (away & (low - 1)) * high + (away >> (low.bit_length() - 1))
        slot = place * bucket + batch_index * capacity + rank
        hit = lax.broadcasted_iota(jnp.int32, (slots, rows), 0) == slot
        placer_ref[:, batch_index * rows : (batch_index + 1) * rows] = jnp.where(
            hit, 1.0, 0.0
        ).astype(jnp.bfloat16)
    for kind in range(2):
        placed = jnp.dot(
            placer_ref[...], rows_refs[kind][...], preferred_element_type=jnp.float32
        ).astype(jnp.bfloat16)
        here_refs[kind][...] = placed[:piece]
        for direct_ref, step in zip(direct_refs, direct_steps):
            direct_ref[:, kind * width : (kind + 1) * width] = placed[
                step * bucket : (step + 1) * bucket
            ]
        for step in range(1, low):
            near_refs[kind * (low - 1) + step - 1][...] = placed[
                step * piece : (step + 1) * piece
            ]


def body(cell_rows, cotangent, cluster_ids, enc_weight, up_weight, down_weight):
    experts = lax.axis_size("expert")
    dp_count = lax.axis_size("dp")
    me = lax.axis_index("expert")
    batch_count, local_rows, model_width = cell_rows.shape
    capacity = max(2, local_rows // 16)
    bucket = batch_count * capacity
    slot_count = experts * bucket
    all_rows = batch_count * local_rows
    high = min(4, experts)
    low = experts // high
    w_up = up_weight[0]
    w_down = down_weight[0]
    fence = lax.optimization_barrier

    vmem = pl.BlockSpec(memory_space=pltpu.VMEM)
    direct_steps = sorted({1, high - 1}, reverse=True)
    shapes = [(high * bucket, model_width)] * (2 * low)
    shapes += [(bucket, 2 * model_width)] * len(direct_steps)
    placed = pl.pallas_call(
        functools.partial(place_kernel, experts, low, high, capacity, direct_steps),
        out_shape=[jax.ShapeDtypeStruct(shape, jnp.bfloat16) for shape in shapes],
        in_specs=[pl.BlockSpec(memory_space=pltpu.SMEM), vmem, vmem, vmem],
        out_specs=[vmem] * len(shapes),
        scratch_shapes=[pltpu.VMEM((slot_count, all_rows), jnp.bfloat16)],
    )(
        me.astype(jnp.int32)[None],
        cluster_ids[:, :, 0],
        cell_rows.reshape(all_rows, model_width),
        cotangent.reshape(all_rows, model_width),
    )
    here, placed = placed[:2], placed[2:]
    cells_placed, grads_placed = placed[: low - 1], list(placed[low - 1 : 2 * (low - 1)])
    direct_placed = placed[2 * (low - 1) :]

    def copies(rows):
        pieces = []
        for shift in range(1, dp_count):
            ring = [(i, (i + shift) % dp_count) for i in range(dp_count)]
            pieces.append(lax.ppermute(rows, "dp", ring))
        return pieces

    def forward(features):
        pre_enc = jnp.dot(features, enc_weight, preferred_element_type=jnp.float32)
        silu_enc, slope_enc = silu_pair(pre_enc)
        encoded = features.astype(jnp.float32) + silu_enc
        inverse = lax.rsqrt(jnp.mean(encoded * encoded, axis=1, keepdims=True) + epsilon)
        norm_rows = (encoded * inverse).astype(jnp.bfloat16)
        pre_exp = jnp.dot(norm_rows, w_up, preferred_element_type=jnp.float32)
        silu_exp, slope_exp = silu_pair(pre_exp)
        return encoded, inverse, slope_enc, norm_rows, silu_exp.astype(jnp.bfloat16), slope_exp

    def stack(*pieces):
        return jnp.concatenate(pieces, axis=0)

    def send_near(pieces, first=1):
        return [swap(pieces[step - first], step) for step in range(low - 1, first - 1, -1)]

    def far_pieces(own, near):
        return [
            stack(
                *[
                    piece[step * bucket : (step + 1) * bucket]
                    for piece in (near if step in direct_steps else [own] + near)
                ]
            )
            for step in range(high - 1, 0, -1)
        ]

    def send_far(pieces):
        return [swap(piece, step * low) for piece, step in zip(pieces, range(high - 1, 0, -1))]

    def here_and_near(own, near):
        pieces = [piece[:bucket] for piece in [own] + near]
        return pieces[0::2], pieces[1::2]

    cells_near = send_near(cells_placed)
    direct_placed, grads_placed[0], cells_near[-1] = fence(
        (direct_placed, grads_placed[0], cells_near[-1])
    )
    grads_near_last = swap(grads_placed[0], 1)
    direct = [swap(piece, step * low) for piece, step in zip(direct_placed, direct_steps)]
    cells_near, direct, here, grads_placed, grads_near_last = fence(
        (cells_near, direct, here, grads_placed[1:], grads_near_last)
    )
    beside = [jnp.concatenate(pair, axis=1) for pair in zip(*here_and_near(here[0], cells_near))]
    first, cells_far, grads_placed, grads_near_last = fence(
        (
            stack(*beside, *direct),
            far_pieces(here[0], cells_near),
            grads_placed,
            grads_near_last,
        )
    )
    first_copies = copies(first)
    grads_near = send_near(grads_placed, 2) + [grads_near_last]
    evens, odds = here_and_near(here[1], grads_near)
    second = stack(*evens, *odds)
    second_copies = copies(second)
    cells_far[-1], second_copies = fence((cells_far[-1], second_copies))
    cells_far = send_far(cells_far)
    grads_far = far_pieces(here[1], grads_near)
    cells_far[:-1], grads_far = fence((cells_far[:-1], grads_far))
    grads_far = send_far(grads_far)
    came = (first_copies, second_copies)
    cells_far, came = fence((cells_far, came))
    cells_far, came = fence((stack(*cells_far), came))
    cells_far_copies = copies(cells_far)

    def unpacked(first, second):
        above = low // 2 * bucket
        left, right = first[:, :model_width], first[:, model_width:]
        return stack(left[:above], right[:above], left[above:]), stack(second, right[above:])

    own_early = unpacked(first, second)
    early = [unpacked(*pair) for pair in zip(*came)]
    features = stack(own_early[0], cells_far)
    grads_far, early, own_forward = fence((grads_far, early, forward(features)))
    grads_far, early, own_forward, features = fence(
        (stack(*grads_far), early, own_forward, features)
    )
    grads_far_copies = copies(grads_far)

    share = model_width // dp_count
    start = lax.axis_index("dp") * share
    block = share // experts

    def my_columns(rows):
        return lax.dynamic_slice_in_dim(rows, start, share, axis=1)

    stages = low.bit_length() - 1
    column = jnp.arange(share, dtype=jnp.int32)
    rank = column // block
    away = rank & (high - 1)
    away = away << stages
    for stage in range(stages):
        away = away | (((rank // high) >> (stages - 1 - stage)) & 1) << stage
    wanted = start + (away ^ me) * block + column % block
    picker = (jnp.arange(model_width, dtype=jnp.int32)[:, None] == wanted[None, :]).astype(
        jnp.bfloat16
    )

    norm_parts, pre_grad_parts, active_parts, grad_parts = [], [], [], []
    enc_parts = []

    def backward(features, grad_rows, values):
        encoded, inverse, slope_enc, norm_rows, active, slope_exp = values
        act_grad = jnp.dot(grad_rows, w_down, preferred_element_type=jnp.float32)
        pre_grad = (act_grad * slope_exp).astype(jnp.bfloat16)
        norm_grad = lax.dot_general(
            pre_grad, w_up, contract_last, preferred_element_type=jnp.float32
        )
        enc_rows_grad = inverse * norm_grad - inverse * inverse * inverse * encoded * jnp.mean(
            norm_grad * encoded, axis=1, keepdims=True
        )
        enc_pre_grad = (enc_rows_grad * slope_enc).astype(jnp.bfloat16)
        picked = jnp.dot(features, picker, preferred_element_type=jnp.float32).astype(jnp.bfloat16)
        enc_parts.append((picked, enc_pre_grad))
        norm_parts.append(my_columns(norm_rows))
        pre_grad_parts.append(pre_grad)
        active_parts.append(active)
        grad_parts.append(my_columns(grad_rows))

    backward(features, stack(own_early[1], grads_far), own_forward)
    cells_far_copies, enc_parts[0] = fence((cells_far_copies, enc_parts[0]))
    for (cells_early, grads_early), cells_far, grads_far in zip(
        early, cells_far_copies, grads_far_copies
    ):
        features = stack(cells_early, cells_far)
        backward(features, stack(grads_early, grads_far), forward(features))

    def enc_terms(first, last):
        total = None
        for picked, enc_pre_grad in enc_parts:
            term = lax.dot_general(
                picked[:, first:last],
                enc_pre_grad,
                contract_rows,
                preferred_element_type=jnp.float32,
            )
            total = term if total is None else total + term
        return total

    kept = share
    total = None
    for stage in range(stages):
        kept //= 2
        if total is None:
            sent, total = enc_terms(kept, 2 * kept), enc_terms(0, kept)
        else:
            sent, total = total[kept:], total[:kept]
        total = total + swap(sent.astype(jnp.bfloat16), 1 << stage).astype(jnp.float32)
    if total is None:
        total = enc_terms(0, share)
    sent = total.astype(jnp.bfloat16)
    total = total[:block]
    for step in range(1, high):
        piece = sent[step * block : (step + 1) * block]
        total = total + swap(piece, step * low).astype(jnp.float32)

    def rows_product(left, right):
        return lax.dot_general(
            jnp.concatenate(left, axis=0),
            jnp.concatenate(right, axis=0),
            contract_rows,
            preferred_element_type=jnp.float32,
        ).astype(jnp.bfloat16)

    up_sum = rows_product(norm_parts, pre_grad_parts)
    down_sum = rows_product(grad_parts, active_parts)
    return (total, up_sum[None], down_sum[None])


def solution(mesh):
    in_specs = (
        P(None, ("dp", "expert"), None),
        P(None, ("dp", "expert"), None),
        P(None, ("dp", "expert"), None),
        P(),
        P("expert", None, None),
        P("expert", None, None),
    )
    out_specs = (P(("dp", "expert"), None), P("expert", "dp", None), P("expert", "dp", None))
    return jax.shard_map(body, mesh=mesh, in_specs=in_specs, out_specs=out_specs, check_vma=False)
```

```python
import functools

import jax
import jax.numpy as jnp
from jax import lax
from jax.experimental import pallas as pl
from jax.experimental.pallas import tpu as pltpu
from jax.sharding import PartitionSpec as P

epsilon = 1e-06
contract_rows = (((0,), (0,)), ((), ()))
contract_last = (((1,), (1,)), ((), ()))


def silu_pair(pre_value):
    gate_value = jax.nn.sigmoid(pre_value)
    return (pre_value * gate_value, gate_value * (1.0 + pre_value * (1.0 - gate_value)))


def swap(piece, distance):
    pairs = [(i, i ^ distance) for i in range(lax.axis_size("expert"))]
    return lax.ppermute(piece, "expert", pairs)


def place_kernel(experts, low, high, capacity, direct_steps, me_ref, ids_ref, *refs):
    rows_refs, here_refs, refs = refs[:2], refs[2:4], refs[4:]
    near_refs, direct_refs, placer_ref = refs[: 2 * (low - 1)], refs[2 * (low - 1) : -1], refs[-1]
    batches, rows = ids_ref.shape
    width = rows_refs[0].shape[1]
    bucket = batches * capacity
    piece = high * bucket
    slots = experts * bucket
    earlier = (
        lax.broadcasted_iota(jnp.int32, (rows, rows), 0)
        < lax.broadcasted_iota(jnp.int32, (rows, rows), 1)
    )
    earlier = jnp.where(earlier, 1.0, 0.0).astype(jnp.bfloat16)
    for batch_index in range(batches):
        label = ids_ref[batch_index : batch_index + 1, :]
        named = lax.broadcasted_iota(jnp.int32, (experts, rows), 0) == label
        onehot = jnp.where(named, 1.0, 0.0)
        before = jnp.dot(onehot.astype(jnp.bfloat16), earlier, preferred_element_type=jnp.float32)
        rank = jnp.sum(before * onehot, axis=0, keepdims=True).astype(jnp.int32)
        away = label ^ me_ref[0]
        place = (away & (low - 1)) * high + (away >> (low.bit_length() - 1))
        slot = place * bucket + batch_index * capacity + rank
        hit = lax.broadcasted_iota(jnp.int32, (slots, rows), 0) == slot
        placer_ref[:, batch_index * rows : (batch_index + 1) * rows] = jnp.where(
            hit, 1.0, 0.0
        ).astype(jnp.bfloat16)
    for kind in range(2):
        placed = jnp.dot(
            placer_ref[...], rows_refs[kind][...], preferred_element_type=jnp.float32
        ).astype(jnp.bfloat16)
        here_refs[kind][...] = placed[:piece]
        for direct_ref, step in zip(direct_refs, direct_steps):
            direct_ref[:, kind * width : (kind + 1) * width] = placed[
                step * bucket : (step + 1) * bucket
            ]
        for step in range(1, low):
            near_refs[kind * (low - 1) + step - 1][...] = placed[
                step * piece : (step + 1) * piece
            ]


def body(cell_rows, cotangent, cluster_ids, enc_weight, up_weight, down_weight):
    experts = lax.axis_size("expert")
    dp_count = lax.axis_size("dp")
    me = lax.axis_index("expert")
    batch_count, local_rows, model_width = cell_rows.shape
    capacity = max(2, local_rows // 16)
    bucket = batch_count * capacity
    slot_count = experts * bucket
    all_rows = batch_count * local_rows
    high = min(4, experts)
    low = experts // high
    w_up = up_weight[0]
    w_down = down_weight[0]
    fence = lax.optimization_barrier

    vmem = pl.BlockSpec(memory_space=pltpu.VMEM)
    direct_steps = sorted({1, high - 1}, reverse=True)
    shapes = [(high * bucket, model_width)] * (2 * low)
    shapes += [(bucket, 2 * model_width)] * len(direct_steps)
    placed = pl.pallas_call(
        functools.partial(place_kernel, experts, low, high, capacity, direct_steps),
        out_shape=[jax.ShapeDtypeStruct(shape, jnp.bfloat16) for shape in shapes],
        in_specs=[pl.BlockSpec(memory_space=pltpu.SMEM), vmem, vmem, vmem],
        out_specs=[vmem] * len(shapes),
        scratch_shapes=[pltpu.VMEM((slot_count, all_rows), jnp.bfloat16)],
    )(
        me.astype(jnp.int32)[None],
        cluster_ids[:, :, 0],
        cell_rows.reshape(all_rows, model_width),
        cotangent.reshape(all_rows, model_width),
    )
    here, placed = placed[:2], placed[2:]
    cells_placed, grads_placed = placed[: low - 1], list(placed[low - 1 : 2 * (low - 1)])
    direct_placed = placed[2 * (low - 1) :]

    def copies(rows):
        pieces = []
        for shift in range(1, dp_count):
            ring = [(i, (i + shift) % dp_count) for i in range(dp_count)]
            pieces.append(lax.ppermute(rows, "dp", ring))
        return pieces

    def forward(features):
        pre_enc = jnp.dot(features, enc_weight, preferred_element_type=jnp.float32)
        silu_enc, slope_enc = silu_pair(pre_enc)
        encoded = features.astype(jnp.float32) + silu_enc
        inverse = lax.rsqrt(jnp.mean(encoded * encoded, axis=1, keepdims=True) + epsilon)
        norm_rows = (encoded * inverse).astype(jnp.bfloat16)
        pre_exp = jnp.dot(norm_rows, w_up, preferred_element_type=jnp.float32)
        silu_exp, slope_exp = silu_pair(pre_exp)
        return encoded, inverse, slope_enc, norm_rows, silu_exp.astype(jnp.bfloat16), slope_exp

    def stack(*pieces):
        return jnp.concatenate(pieces, axis=0)

    def send_near(pieces, first=1):
        return [swap(pieces[step - first], step) for step in range(low - 1, first - 1, -1)]

    def far_pieces(own, near):
        return [
            stack(
                *[
                    piece[step * bucket : (step + 1) * bucket]
                    for piece in (near if step in direct_steps else [own] + near)
                ]
            )
            for step in range(high - 1, 0, -1)
        ]

    def send_far(pieces):
        return [swap(piece, step * low) for piece, step in zip(pieces, range(high - 1, 0, -1))]

    def here_and_near(own, near):
        return stack(*[piece[:bucket] for piece in [own] + near])

    cells_near = send_near(cells_placed)
    direct_placed, grads_placed[0], cells_near[-1] = fence(
        (direct_placed, grads_placed[0], cells_near[-1])
    )
    grads_near_last = swap(grads_placed[0], 1)
    direct = [swap(piece, step * low) for piece, step in zip(direct_placed, direct_steps)]
    cells_near, direct, here, grads_placed, grads_near_last = fence(
        (cells_near, direct, here, grads_placed[1:], grads_near_last)
    )
    cells_first, direct, cells_far, grads_placed, grads_near_last = fence(
        (
            here_and_near(here[0], cells_near),
            stack(*direct),
            far_pieces(here[0], cells_near),
            grads_placed,
            grads_near_last,
        )
    )
    cells_first_copies = copies(cells_first)
    grads_near = send_near(grads_placed, 2) + [grads_near_last]
    cells_far[-1], cells_first_copies = fence((cells_far[-1], cells_first_copies))
    cells_far = send_far(cells_far)
    direct_cells, direct_grads = direct[:, :model_width], direct[:, model_width:]
    grads_first = here_and_near(here[1], grads_near)
    second_copies = copies(stack(grads_first, direct_cells, direct_grads))
    grads_far = far_pieces(here[1], grads_near)
    cells_far[:-1], grads_far = fence((cells_far[:-1], grads_far))
    grads_far = send_far(grads_far)
    came = (cells_first_copies, second_copies)
    cells_far, came = fence((cells_far, came))
    cells_far, came = fence((stack(*cells_far), came))
    cells_far_copies = copies(cells_far)
    features = stack(cells_first, direct_cells, cells_far)
    first_rows, direct_rows = cells_first.shape[0], direct.shape[0]
    early = [
        (
            stack(cells, second[first_rows:-direct_rows]),
            stack(second[:first_rows], second[-direct_rows:]),
        )
        for cells, second in zip(*came)
    ]
    grads_far, early, own_forward = fence((grads_far, early, forward(features)))
    grads_far, early, own_forward, features = fence(
        (stack(*grads_far), early, own_forward, features)
    )
    grads_far_copies = copies(grads_far)

    share = model_width // dp_count
    start = lax.axis_index("dp") * share
    block = share // experts

    def my_columns(rows):
        return lax.dynamic_slice_in_dim(rows, start, share, axis=1)

    stages = low.bit_length() - 1
    column = jnp.arange(share, dtype=jnp.int32)
    rank = column // block
    away = rank & (high - 1)
    away = away << stages
    for stage in range(stages):
        away = away | (((rank // high) >> (stages - 1 - stage)) & 1) << stage
    wanted = start + (away ^ me) * block + column % block
    picker = (jnp.arange(model_width, dtype=jnp.int32)[:, None] == wanted[None, :]).astype(
        jnp.bfloat16
    )

    norm_parts, pre_grad_parts, active_parts, grad_parts = [], [], [], []
    enc_parts = []

    def backward(features, grad_rows, values):
        encoded, inverse, slope_enc, norm_rows, active, slope_exp = values
        act_grad = jnp.dot(grad_rows, w_down, preferred_element_type=jnp.float32)
        pre_grad = (act_grad * slope_exp).astype(jnp.bfloat16)
        norm_grad = lax.dot_general(
            pre_grad, w_up, contract_last, preferred_element_type=jnp.float32
        )
        enc_rows_grad = inverse * norm_grad - inverse * inverse * inverse * encoded * jnp.mean(
            norm_grad * encoded, axis=1, keepdims=True
        )
        enc_pre_grad = (enc_rows_grad * slope_enc).astype(jnp.bfloat16)
        picked = jnp.dot(features, picker, preferred_element_type=jnp.float32).astype(jnp.bfloat16)
        enc_parts.append((picked, enc_pre_grad))
        norm_parts.append(my_columns(norm_rows))
        pre_grad_parts.append(pre_grad)
        active_parts.append(active)
        grad_parts.append(my_columns(grad_rows))

    backward(features, stack(grads_first, direct_grads, grads_far), own_forward)
    cells_far_copies, enc_parts[0] = fence((cells_far_copies, enc_parts[0]))
    for (cells_early, grads_early), cells_far, grads_far in zip(
        early, cells_far_copies, grads_far_copies
    ):
        features = stack(cells_early, cells_far)
        backward(features, stack(grads_early, grads_far), forward(features))

    def enc_terms(first, last):
        total = None
        for picked, enc_pre_grad in enc_parts:
            term = lax.dot_general(
                picked[:, first:last],
                enc_pre_grad,
                contract_rows,
                preferred_element_type=jnp.float32,
            )
            total = term if total is None else total + term
        return total

    kept = share
    total = None
    for stage in range(stages):
        kept //= 2
        if total is None:
            sent, total = enc_terms(kept, 2 * kept), enc_terms(0, kept)
        else:
            sent, total = total[kept:], total[:kept]
        total = total + swap(sent.astype(jnp.bfloat16), 1 << stage).astype(jnp.float32)
    if total is None:
        total = enc_terms(0, share)
    sent = total.astype(jnp.bfloat16)
    total = total[:block]
    for step in range(1, high):
        piece = sent[step * block : (step + 1) * block]
        total = total + swap(piece, step * low).astype(jnp.float32)

    def rows_product(left, right):
        return lax.dot_general(
            jnp.concatenate(left, axis=0),
            jnp.concatenate(right, axis=0),
            contract_rows,
            preferred_element_type=jnp.float32,
        ).astype(jnp.bfloat16)

    up_sum = rows_product(norm_parts, pre_grad_parts)
    down_sum = rows_product(grad_parts, active_parts)
    return (total, up_sum[None], down_sum[None])


def solution(mesh):
    in_specs = (
        P(None, ("dp", "expert"), None),
        P(None, ("dp", "expert"), None),
        P(None, ("dp", "expert"), None),
        P(),
        P("expert", None, None),
        P("expert", None, None),
    )
    out_specs = (P(("dp", "expert"), None), P("expert", "dp", None), P("expert", "dp", None))
    return jax.shard_map(body, mesh=mesh, in_specs=in_specs, out_specs=out_specs, check_vma=False)
```
